128 devices in a mesh: wide: 16 (over x, y), narrow: 8 (over z, core).
Axes of the slice: x: 4, y: 4, z: 4, core: 2. Of those that a mesh axis runs over, the one named last changes fastest.
Arguments:
- classes: float32 [32, 256, 128, 128], P(None, 'wide', 'narrow'), may hold values from 0.1 to 2
- velocity: float32 [3, 256, 128, 128], P(None, 'wide', 'narrow'), may hold values from -0.3 to 0.3
- attach_rate: float32 [32], replicated, may hold values from 0.05 to 1
- bubble_pos: float32 [12288, 3, 128], P(('wide', 'narrow')), may hold values from 0 to 1
- bubble_volume: float32 [12288, 128], P(('wide', 'narrow')), may hold values from 0.05 to 0.5
- bubble_area: float32 [12288, 128], P(('wide', 'narrow')), may hold values from 0.2 to 2
- bubble_count: int32 [1536, 8], P(('wide', 'narrow')), may hold values from 1 to 128, 640 in all within a row
- cluster_target: int32 [12288, 1], P(('wide', 'narrow')), may hold values from 0 to 127; in each aligned block of 96 rows (0 to 95, 96 to 191, ...) at most 2 rows name the same one
- cluster_offset: int32 [12288, 2], P(('wide', 'narrow')), may hold values from 0 to 12
Outputs:
- deposit: float32 [2, 256, 128, 128], P(None, 'wide', 'narrow')
- transported: float32 [32, 256, 128, 128], P(None, 'wide', 'narrow')
The draws below stay inside these ranges and needn't reach their ends.
Inputs may be any that keep to these rules, and one draw needn't show every extreme that they name: `cluster_target`: within the clusters listed on one device no brick is named more than 2 times, a bound that some block reaches. `bubble_count`: the counts of each row of 8 sum to 640; some cluster of each row is full.
All inputs are finite; a program needn't handle non-finite values.
Results may differ from the reference program's by a relative error of at most 0.0001.
Values sent between devices are 32-bit elements; how exact they have to be, the bound alone decides.
No kernel may reach another device: no remote copies, remote signals or barrier semaphores. Data moves between devices by JAX's collectives and lax.ppermute only.
A program may use at most 128 MiB of HBM per device.

```python
import math
import jax
import jax.numpy as jnp
import numpy as np
from jax import lax

BRICK = 16
NZ = 128
K = 32
BUB = 128
WIN = 4
STEPS = 4
CL_DEV = 96
CAP = 2
CLUSTERS = 12288
NX = 256
NY = 128
N_WIDE = 16
N_NARROW = 8


def touch_ends(values, own_key, low, top_value):
    index_at = [jax.random.randint(jax.random.fold_in(own_key, axis), (), 0, length) for axis, length in enumerate(values.shape)]
    widest = values.shape.index(max(values.shape))
    next_to = index_at[:widest] + [(index_at[widest] + 1) % values.shape[widest]] + index_at[widest + 1:]
    return values.at[tuple(index_at)].set(low).at[tuple(next_to)].set(top_value)


def block_scale(key, dims, split, low, top_value):
    loudness, own = 1.0, jax.random.fold_in(key, 6)
    for axis_at, parts in split:
        steps = jnp.exp(jax.random.uniform(jax.random.fold_in(own, axis_at), (parts,), jnp.float32, low / len(split), top_value / len(split)))
        loudness = loudness * jnp.repeat(steps, dims[axis_at] // parts).reshape([-1 if axis == axis_at else 1 for axis in range(len(dims))])
    return loudness


def profile(amount, total, bound, lean):
    loads = [(1 << 20) // math.isqrt(standing ** lean) + 1 for standing in range(2, amount + 1)]
    surplus, holding = total - bound - (amount - 1), [1] * (amount - 1)
    while surplus > 0:
        movable = [i for i in range(amount - 1) if holding[i] < bound]
        pool, remaining = sum([loads[i] for i in movable]), surplus
        for i in movable:
            addition = min(bound - holding[i], max(1, remaining * loads[i] // pool), surplus)
            holding[i] = holding[i] + addition
            surplus = surplus - addition
    return np.array([bound] + holding)


def uneven(stream_key, count, total, bound, slope):
    if count == 2:
        one = jax.random.randint(stream_key, (), max(1, total - bound), min(bound, total - 1) + 1)
        return jnp.stack([one, total - one])
    lengths = jnp.asarray(profile(count, total, bound, slope), jnp.int32)
    pairs = (count - 1) // 2
    source_of, receiver = lengths[1:1 + 2 * pairs:2], lengths[2:2 + 2 * pairs:2]
    slack = jnp.minimum(source_of - 1, bound - receiver)
    passed = jax.random.randint(jax.random.fold_in(stream_key, 1), (pairs,), 0, 1 << 20) % (slack + 1)
    lengths = lengths.at[1:1 + 2 * pairs:2].set(source_of - passed).at[2:2 + 2 * pairs:2].set(receiver + passed)
    return lengths[jax.random.permutation(jax.random.fold_in(stream_key, 2), count)]


def routed_block(rng, own, number, rows, count, top, reach, slope):
    sequence = jax.random.permutation(rng, count)
    crowded, ordinary = shares(count, rows * top, reach, slope, True), shares(count, rows * top, reach, slope, False)
    places = jnp.arange(count)

    def named(tallies, rotation):
        used = int((tallies > 0).sum())
        fixed = max(1, used // 4)
        passed = fixed + (places - fixed + rotation * (used - fixed)) % max(1, count - fixed)
        return jnp.zeros((count,), jnp.int32).at[sequence[jnp.where(places < fixed, places, passed)]].set(jnp.asarray(tallies, jnp.int32))

    tallies = jnp.where(number % 4 == 0, named(crowded, number // 4), named(ordinary, number - number // 4 - 1))
    mixed = jax.random.permutation(jax.random.fold_in(own, 3), count)
    donor, receiver = mixed[0:count // 2 * 2:2], mixed[1:count // 2 * 2:2]
    margin = jnp.minimum(tallies[donor] - 1, reach - tallies[receiver]) // 2
    margin = jnp.where((donor == sequence[0]) | (receiver == sequence[0]) | (tallies[receiver] == 0), 0, jnp.maximum(margin, 0))
    passed = jax.random.randint(jax.random.fold_in(own, 4), (count // 2,), 0, 1 << 20) % (margin + 1)
    tallies = tallies.at[donor].add(-passed).at[receiver].add(passed)
    items = jnp.searchsorted(jnp.cumsum(tallies), jnp.arange(rows * top), side="right").astype(jnp.int32)
    listing = items.reshape(top, rows).T
    listing = listing[jax.random.permutation(jax.random.fold_in(own, 1), rows)]
    rotation = jax.random.randint(jax.random.fold_in(own, 2), (rows, 1), 0, top)
    return jnp.take_along_axis(listing, (jnp.arange(top)[None, :] + rotation) % top, axis=1)


def shares(amount, total, most, slope, full):
    portions = [(1 << 20) // math.isqrt(grade ** slope) + 1 for grade in range(1, amount + 1)]
    largest = most if full else min(most, max(-(-total // amount), total * portions[0] // sum(portions)))
    least = 1 if total - largest >= amount - 1 else 0
    holding, surplus = [largest] + [least] * (amount - 1), total - largest - least * (amount - 1)
    while surplus > 0:
        candidates = [i for i in range(1, amount) if holding[i] < largest] or [i for i in range(1, amount) if holding[i] < most]
        whole, left = sum([portions[i] for i in candidates]), surplus
        for i in candidates:
            extra = min(most - holding[i], max(1, left * portions[i] // whole), surplus)
            holding[i] = holding[i] + extra
            surplus = surplus - extra
    return np.array(holding)


def setup_inputs(seed: int = 0) -> dict:
    splits = jax.random.split(jax.random.key(seed), 10)
    classes = jnp.clip(jnp.exp(math.log(2.0) - 2.9957323 * jax.random.uniform(splits[0], (K, NX, NY, NZ), jnp.float32) ** block_scale(splits[0], (K, NX, NY, NZ), ((1, 16), (2, 8)), -0.2, 0.2)), 0.1, 2.0)
    velocity = jnp.clip(jax.random.uniform(splits[1], (3, NX, NY, NZ), jnp.float32, -0.3, 0.3) * block_scale(splits[1], (3, NX, NY, NZ), ((1, 16), (2, 8)), -0.4, 0.0), -0.3, 0.3)
    attach_rate = jnp.clip(jnp.exp(jax.random.uniform(splits[2], (K,), jnp.float32, math.log(0.05), math.log(1.0))), 0.05, 1.0)
    bubble_pos = jnp.clip(1.0 * jax.random.uniform(splits[3], (CLUSTERS, 3, BUB), jnp.float32) ** block_scale(splits[3], (CLUSTERS, 3, BUB), ((0, 128),), -0.2, 0.2), 0.0, 1.0)
    bubble_volume = jnp.clip(jnp.exp(math.log(0.5) - 2.3025851 * jax.random.uniform(splits[4], (CLUSTERS, BUB), jnp.float32) ** block_scale(splits[4], (CLUSTERS, BUB), ((0, 128),), -0.2, 0.2)), 0.05, 0.5)
    bubble_area = jnp.clip(jnp.exp(math.log(2.0) - 2.3025851 * jax.random.uniform(splits[5], (CLUSTERS, BUB), jnp.float32) ** block_scale(splits[5], (CLUSTERS, BUB), ((0, 128),), -0.2, 0.2)), 0.2, 2.0)
    bubble_count = jax.vmap(lambda own: uneven(own, 8, 640, BUB, 1))(jax.random.split(splits[6], (CLUSTERS // 8))).reshape((CLUSTERS // 8, 8)).astype(jnp.int32)
    cluster_target_keys = jax.random.split(jax.random.fold_in(splits[7], 1), CLUSTERS // CL_DEV)
    cluster_target_turns = jax.random.permutation(jax.random.fold_in(splits[7], 3), CLUSTERS // CL_DEV)
    cluster_target = jax.vmap(lambda own, number: routed_block(jax.random.fold_in(splits[7], 2), own, number, CL_DEV, N_WIDE * N_NARROW, 1, CAP, 2))(cluster_target_keys, cluster_target_turns).reshape((CLUSTERS, 1))
    cluster_offset = touch_ends(jax.random.randint(splits[8], (CLUSTERS, 2), 0, BRICK - WIN + 1), jax.random.fold_in(splits[8], 1), 0, BRICK - WIN).astype(jnp.int32)
    return dict(classes=classes, velocity=velocity, attach_rate=attach_rate, bubble_pos=bubble_pos, bubble_volume=bubble_volume, bubble_area=bubble_area, bubble_count=bubble_count, cluster_target=cluster_target, cluster_offset=cluster_offset)


spread_var = 1.0


def kernels(bubble_pos, volume, area_rows, window, depth_cells):
    slots_here = bubble_pos.shape[0]
    bubbles = bubble_pos.shape[2]
    across = jnp.arange(window, dtype=jnp.float32) + 0.5
    along_z = jnp.arange(depth_cells, dtype=jnp.float32) + 0.5
    centre_x = bubble_pos[:, 0, :] * window
    centre_y = bubble_pos[:, 1, :] * window
    centre_z = bubble_pos[:, 2, :] * depth_cells
    twice_var = 2.0 * spread_var
    kernel_x = jnp.exp(-((across[None, :, None] - centre_x[:, None, :]) ** 2) / twice_var)
    kernel_y = jnp.exp(-((across[None, :, None] - centre_y[:, None, :]) ** 2) / twice_var)
    kernel_z = jnp.exp(-((along_z[None, None, :] - centre_z[:, :, None]) ** 2) / twice_var)
    plane_kernel = (kernel_x[:, :, None, :] * kernel_y[:, None, :, :]).reshape(slots_here, window * window, bubbles)
    load_rows = jnp.concatenate([volume[:, :, None] * kernel_z, area_rows[:, :, None] * kernel_z], axis=2)
    return jnp.einsum("smb,sbn->smn", plane_kernel, load_rows, precision=lax.Precision.HIGHEST)


def windows_of(bubble_pos, volume, area_rows, window, depth_cells):
    total_rows = bubble_pos.shape[0]
    block_rows = math.gcd(total_rows, 32)
    count_blocks = total_rows // block_rows

    def block_kernels(packed):
        return kernels(packed[0], packed[1], packed[2], window, depth_cells)

    stacked = lax.map(block_kernels, (bubble_pos.reshape((count_blocks, block_rows) + bubble_pos.shape[1:]), volume.reshape(count_blocks, block_rows, volume.shape[1]), area_rows.reshape(count_blocks, block_rows, area_rows.shape[1])))
    return stacked.reshape(total_rows, window * window, 2 * depth_cells)


def advect(padded, vel_pad):
    field_z = jnp.pad(padded, [(0, 0)] * (padded.ndim - 1) + [(1, 1)])
    speed_z = jnp.pad(vel_pad, ((0, 0), (0, 0), (0, 0), (1, 1)))
    centre = field_z[..., 1:-1, 1:-1, 1:-1]
    left_cells = field_z[..., :-1, 1:-1, 1:-1]
    right_cells = field_z[..., 1:, 1:-1, 1:-1]
    face_speed = 0.5 * (speed_z[0, :-1, 1:-1, 1:-1] + speed_z[0, 1:, 1:-1, 1:-1])
    flux_x = jnp.maximum(face_speed, 0.0) * left_cells + jnp.minimum(face_speed, 0.0) * right_cells
    left_cells = field_z[..., 1:-1, :-1, 1:-1]
    right_cells = field_z[..., 1:-1, 1:, 1:-1]
    face_speed = 0.5 * (speed_z[1, 1:-1, :-1, 1:-1] + speed_z[1, 1:-1, 1:, 1:-1])
    flux_y = jnp.maximum(face_speed, 0.0) * left_cells + jnp.minimum(face_speed, 0.0) * right_cells
    left_cells = field_z[..., 1:-1, 1:-1, :-1]
    right_cells = field_z[..., 1:-1, 1:-1, 1:]
    face_speed = 0.5 * (speed_z[2, 1:-1, 1:-1, :-1] + speed_z[2, 1:-1, 1:-1, 1:])
    flux_z = jnp.maximum(face_speed, 0.0) * left_cells + jnp.minimum(face_speed, 0.0) * right_cells
    change = flux_x[..., 1:, :, :] - flux_x[..., :-1, :, :]
    change = change + flux_y[..., :, 1:, :] - flux_y[..., :, :-1, :]
    change = change + flux_z[..., 1:] - flux_z[..., :-1]
    return centre - change


def reference(classes, velocity, attach_rate, bubble_pos, bubble_volume, bubble_area, bubble_count, cluster_target, cluster_offset):
    cluster_total = bubble_pos.shape[0]
    live_mask = (jnp.arange(BUB, dtype=jnp.int32)[None, :] < bubble_count.reshape(-1)[:, None]).astype(jnp.float32)
    windows = windows_of(bubble_pos, bubble_volume * live_mask, bubble_area * live_mask, WIN, NZ)
    target = cluster_target[:, 0]
    base_x = (target // N_NARROW) * BRICK + cluster_offset[:, 0]
    base_y = (target % N_NARROW) * BRICK + cluster_offset[:, 1]
    window_steps = jnp.arange(WIN, dtype=jnp.int32)
    index_x = jnp.broadcast_to(base_x[:, None, None] + window_steps[None, :, None], (cluster_total, WIN, WIN)).astype(jnp.int32)
    index_y = jnp.broadcast_to(base_y[:, None, None] + window_steps[None, None, :], (cluster_total, WIN, WIN)).astype(jnp.int32)
    grid_sum = jnp.zeros((NX, NY, 2 * NZ), jnp.float32).at[index_x, index_y].add(windows.reshape(cluster_total, WIN, WIN, 2 * NZ))
    deposit = jnp.transpose(grid_sum.reshape(NX, NY, 2, NZ), (2, 0, 1, 3))
    attach_load = deposit[1] / (1.0 + deposit[0])
    vel_pad = jnp.pad(velocity, ((0, 0), (1, 1), (1, 1), (0, 0)))

    def one_class(packed):
        field_now, class_rate = packed
        factor = jnp.exp(-class_rate * attach_load)
        for substep in range(STEPS):
            padded = jnp.pad(field_now, ((1, 1), (1, 1), (0, 0)))
            field_now = advect(padded, vel_pad) * factor
        return field_now

    transported = lax.map(one_class, (classes, attach_rate))
    return deposit, transported
```

```python
import functools

import jax
import jax.numpy as jnp
from jax import lax
from jax.experimental import pallas as pl
from jax.experimental.pallas import tpu as pltpu
from jax.sharding import PartitionSpec as P

WIN = 4
DEPTH = 4
GROUP = 8
AXES = ("wide", "narrow")
VMEM_BYTES = 60 * 1024 * 1024

CORNER = [(a, b) for a in range(DEPTH - 1) for b in range(DEPTH - 1 - a)]


def params(**more):
    return pltpu.CompilerParams(vmem_limit_bytes=VMEM_BYTES, **more)


def rolled(block, wide_step, narrow_step):
    wide_count, narrow_count = lax.axis_size("wide"), lax.axis_size("narrow")
    pairs = [
        (
            w * narrow_count + n,
            (w + wide_step) % wide_count * narrow_count + (n + narrow_step) % narrow_count,
        )
        for w in range(wide_count)
        for n in range(narrow_count)
    ]
    return lax.ppermute(block, AXES, pairs)


def pack_kernel(meta, pos, volume, area, sent, tally):
    clusters, _, bubbles = pos.shape
    devices = sent.shape[0]
    sent[...] = jnp.zeros_like(sent)

    def clear(d, carry):
        tally[d] = 0
        return carry

    lax.fori_loop(0, devices, clear, 0)
    lane = lax.broadcasted_iota(jnp.int32, (1, bubbles), 1)

    def one(c, carry):
        target, count = meta[c], meta[clusters + c]
        corner_x = meta[2 * clusters + c].astype(jnp.float32)
        corner_y = meta[3 * clusters + c].astype(jnp.float32)
        rank = tally[target]
        tally[target] = rank + 1
        base = rank * (5 * bubbles)
        live = lane < count
        rows = [
            pos[c, 0:1, :] * 4.0,
            pos[c, 1:2, :] * 4.0,
            pos[c, 2:3, :] * 128.0,
            jnp.where(live, volume[pl.ds(c, 1), :], 0.0),
            jnp.where(live, area[pl.ds(c, 1), :], 0.0),
        ]
        for i, row in enumerate(rows):
            start = pl.multiple_of(base + i * bubbles, bubbles)
            sent[target, :, pl.ds(start, bubbles)] = row
        tail = sent[target, :, pl.ds(10 * bubbles, bubbles)]
        tail = jnp.where(lane == 2 * rank, corner_x, tail)
        tail = jnp.where(lane == 2 * rank + 1, corner_y, tail)
        sent[target, :, pl.ds(10 * bubbles, bubbles)] = tail
        return carry

    lax.fori_loop(0, clusters, one, 0, unroll=4)


def pack(meta, pos, volume, area, devices):
    bubbles = pos.shape[2]
    return pl.pallas_call(
        pack_kernel,
        out_shape=jax.ShapeDtypeStruct((devices, 1, 11 * bubbles), jnp.float32),
        in_specs=[pl.BlockSpec(memory_space=pltpu.SMEM)]
        + [pl.BlockSpec(memory_space=pltpu.VMEM)] * 3,
        out_specs=pl.BlockSpec(memory_space=pltpu.VMEM),
        scratch_shapes=[pltpu.SMEM((devices,), jnp.int32)],
        compiler_params=params(),
    )(meta, pos, volume, area)


UNROLL = 4


def halves(value):
    high = value.astype(jnp.bfloat16)
    return high, (value - high.astype(jnp.float32)).astype(jnp.bfloat16)


def across(left, right):
    return lax.dot_general(
        left, right, (((1,), (1,)), ((), ())), preferred_element_type=jnp.float32
    )


def bell(distance):
    return jnp.exp2((distance * (-0.5 * 1.4426950408889634)) * distance)


def deposit_kernel(got_any, got, deposit, attach, total, corners, sem):
    devices = got.shape[0]
    bubbles = got.shape[2] // 11
    copy = pltpu.make_async_copy(
        got_any.at[:, :, pl.ds(10 * bubbles, bubbles)], corners, sem
    )
    copy.start()
    total[...] = jnp.zeros_like(total)
    copy.wait()
    row = lax.broadcasted_iota(jnp.int32, (8, bubbles), 0)
    is_volume = row % 2 == 0
    cell_y = (row // 2).astype(jnp.float32) + 0.5
    cell_z = lax.broadcasted_iota(jnp.int32, (128, bubbles), 0).astype(jnp.float32) + 0.5

    def sources(step, carry):
        done = []
        for u in range(UNROLL):
            for slot in range(2):
                source = step * UNROLL + u
                px, py, pz, vol, are = (
                    got[source, :, (5 * slot + i) * bubbles : (5 * slot + i + 1) * bubbles]
                    for i in range(5)
                )
                share = bell(cell_y - py) * jnp.where(is_volume, vol, are)
                plane = jnp.concatenate(
                    [share * bell((i + 0.5) - px) for i in range(WIN)], axis=0
                )
                plane_high, plane_low = halves(plane)
                high, low = halves(bell(cell_z - pz))
                both = across(jnp.concatenate([plane_high, plane_low], axis=0), high)
                window = both[:32] + both[32:] + across(plane_high, low)
                done.append((source, slot, window))
        for source, slot, window in done:
            x = corners[source, 0, 2 * slot].astype(jnp.int32)
            y = corners[source, 0, 2 * slot + 1].astype(jnp.int32)
            for i in range(WIN):
                at = pl.ds((x + i) * 32 + y * 2, 8)
                total[at, :] = total[at, :] + window[8 * i : 8 * i + 8]
        return carry

    lax.fori_loop(0, devices // UNROLL, sources, 0)
    for x in range(16):
        gas = total[pl.ds(x * 32, 16, stride=2), :]
        face = total[pl.ds(x * 32 + 1, 16, stride=2), :]
        deposit[0, x] = gas
        deposit[1, x] = face
        attach[x] = face / (1.0 + gas)


def deposited(got):
    devices = got.shape[0]
    return pl.pallas_call(
        deposit_kernel,
        out_shape=(
            jax.ShapeDtypeStruct((2, 16, 16, 128), jnp.float32),
            jax.ShapeDtypeStruct((16, 16, 128), jnp.float32),
        ),
        in_specs=[
            pl.BlockSpec(memory_space=pl.ANY),
            pl.BlockSpec(memory_space=pltpu.VMEM),
        ],
        out_specs=(pl.BlockSpec(memory_space=pltpu.VMEM),) * 2,
        scratch_shapes=[
            pltpu.VMEM((512, 128), jnp.float32),
            pltpu.SMEM((devices, 1, 128), jnp.float32),
            pltpu.SemaphoreType.DMA,
        ],
        compiler_params=params(),
    )(got, got)


WIDE_ROWS = 16 * 32 + 3 * 16
SIDE_ROWS = DEPTH * 32 + 16
CORNER_ROWS = len(CORNER) * 32 + 24


def strips_kernel(classes, velocity, own, wide_low, wide_high, side_low, side_high, *corners):
    x = pl.program_id(0)
    cells = jnp.swapaxes(classes[:, 0], 0, 1)
    speed = velocity[:, 0]
    flat = cells.reshape(16 * 32, 128)
    own[0] = flat

    @pl.when(x < DEPTH)
    def _():
        wide_low[0, 0:512, :] = flat
        wide_low[0, 512:560, :] = speed.reshape(48, 128)

    @pl.when(x >= 16 - DEPTH)
    def _():
        wide_high[0, 0:512, :] = flat
        wide_high[0, 512:560, :] = speed.reshape(48, 128)

    for out, first in ((side_low, 0), (side_high, 16 - DEPTH)):
        out[0, 0:128, :] = flat[first * 32 : (first + DEPTH) * 32]
        for d in range(3):
            out[0, 128 + 4 * d : 132 + 4 * d, :] = speed[d, first : first + DEPTH]
    for at, out in enumerate(corners):
        high_x, high_y = divmod(at, 2)
        for a in range(DEPTH - 1):

            @pl.when(x == (15 - a if high_x else a))
            def _(a=a, high_x=high_x, high_y=high_y, out=out):
                for cell, (this_a, b) in enumerate(CORNER):
                    if this_a == a:
                        y = 15 - b if high_y else b
                        out[cell * 32 : cell * 32 + 32, :] = flat[y * 32 : y * 32 + 32]
                        for d in range(3):
                            at_row = len(CORNER) * 32 + 3 * cell + d
                            out[at_row : at_row + 1, :] = speed[d, y : y + 1]


def strips(classes, velocity):
    def rows(*count):
        return jax.ShapeDtypeStruct(count + (128,), jnp.float32)

    return pl.pallas_call(
        strips_kernel,
        grid=(16,),
        out_shape=(rows(16, 512),)
        + (rows(DEPTH, WIDE_ROWS),) * 2
        + (rows(16, SIDE_ROWS),) * 2
        + (rows(CORNER_ROWS),) * 4,
        in_specs=[
            pl.BlockSpec((32, 1, 16, 128), lambda x: (0, x, 0, 0)),
            pl.BlockSpec((3, 1, 16, 128), lambda x: (0, x, 0, 0)),
        ],
        out_specs=(
            pl.BlockSpec((1, 512, 128), lambda x: (x, 0, 0)),
            pl.BlockSpec((1, WIDE_ROWS, 128), lambda x: (jnp.minimum(x, DEPTH - 1), 0, 0)),
            pl.BlockSpec((1, WIDE_ROWS, 128), lambda x: (jnp.maximum(x - 16 + DEPTH, 0), 0, 0)),
            pl.BlockSpec((1, SIDE_ROWS, 128), lambda x: (x, 0, 0)),
            pl.BlockSpec((1, SIDE_ROWS, 128), lambda x: (x, 0, 0)),
        )
        + (pl.BlockSpec((CORNER_ROWS, 128), lambda x: (0, 0)),) * 4,
        compiler_params=params(),
    )(classes, velocity)


SPAN = 16 + 2 * DEPTH
ORIGIN = 8


def transport_kernel(
    own, wide_low, wide_high, side_low, side_high, c00, c01, c10, c11,
    velocity, attach, attach_low, attach_high, rate,
    out,
    field, other, factor, speed, coef, side_speed, corner_buf, stage,
    sem, out_sem,
):
    corners = (c00, c01, c10, c11)
    copies = []

    def copy(source, target):
        moved = pltpu.make_async_copy(source, target, sem.at[len(copies)])
        moved.start()
        copies.append(moved)

    inner = pl.ds(DEPTH, 16)
    copy(velocity, speed.at[:, inner, pl.ds(ORIGIN, 16)])
    for side, block in enumerate((side_low, side_high)):
        copy(block.at[:, pl.ds(DEPTH * 32, 16)], side_speed.at[side])
    for at, block in enumerate(corners):
        copy(block, corner_buf.at[at])
    for block, first in ((wide_low, 0), (wide_high, 16 + DEPTH)):
        for d in range(3):
            copy(
                block.at[:, pl.ds(512 + 16 * d, 16)],
                speed.at[d, pl.ds(first, DEPTH), pl.ds(ORIGIN, 16)],
            )
    for block, first in ((wide_low, 0), (wide_high, 16 + DEPTH)):
        copy(
            block.at[:, pl.ds(0, 512)],
            field.at[pl.ds(first, DEPTH), pl.ds(DEPTH * 32, 512)],
        )
    for block, first in ((side_low, 0), (side_high, 16 + DEPTH)):
        copy(block.at[:, pl.ds(0, DEPTH * 32)], field.at[inner, pl.ds(first * 32, DEPTH * 32)])
    copy(own, field.at[inner, pl.ds(DEPTH * 32, 512)])
    for moved in copies:
        moved.wait()

    for side, first in ((0, ORIGIN - DEPTH), (1, ORIGIN + 16)):
        for x in range(16):
            for d in range(3):
                speed[d, DEPTH + x, first : first + DEPTH, :] = side_speed[
                    side, x, 4 * d : 4 * d + 4, :
                ]
    for at in range(4):
        high_x, high_y = divmod(at, 2)
        for cell, (a, b) in enumerate(CORNER):
            x = 16 + DEPTH + a if high_x else DEPTH - 1 - a
            y = 16 + DEPTH + b if high_y else DEPTH - 1 - b
            field[x, y * 32 : y * 32 + 32, :] = corner_buf[at, cell * 32 : cell * 32 + 32, :]
            yv = y + ORIGIN - DEPTH
            for d in range(3):
                at_row = len(CORNER) * 32 + 3 * cell + d
                speed[d, x, yv : yv + 1, :] = corner_buf[at, at_row : at_row + 1, :]

    wide_at, narrow_at = lax.axis_index("wide"), lax.axis_index("narrow")
    wide_last, narrow_last = lax.axis_size("wide") - 1, lax.axis_size("narrow") - 1
    edges = (wide_at == 0, wide_at == wide_last, narrow_at == 0, narrow_at == narrow_last)
    spans = ((0, DEPTH), (16 + DEPTH, SPAN))

    def clear(ref, by_rows):
        for side, (first, last) in enumerate(spans):

            @pl.when(edges[side])
            def _(first=first, last=last):
                ref[first:last] = jnp.zeros((last - first,) + ref.shape[1:], jnp.float32)

            @pl.when(edges[2 + side])
            def _(first=first, last=last):
                ref[:, first * by_rows : last * by_rows] = jnp.zeros(
                    (ref.shape[0], (last - first) * by_rows, 128), jnp.float32
                )

    clear(field, 32)
    for side, (first, last) in enumerate(spans):

        @pl.when(edges[side])
        def _(first=first, last=last):
            speed[:, first:last] = jnp.zeros((3, last - first) + speed.shape[2:], jnp.float32)

        @pl.when(edges[2 + side])
        def _(first=first, last=last):
            shift = ORIGIN - DEPTH
            speed[:, :, first + shift : last + shift] = jnp.zeros(
                (3, SPAN, last - first, 128), jnp.float32
            )

    lane = lax.broadcasted_iota(jnp.int32, (SPAN - 2, 128), 1)

    def coefficients(x, carry):
        low, high = ORIGIN - DEPTH + 1, ORIGIN + 16 + DEPTH - 1

        def at(d, dx, dy):
            return speed[d, x + dx, low + dy : high + dy, :]

        middle = [at(d, 0, 0) for d in range(3)]
        left = 0.5 * (at(0, -1, 0) + middle[0])
        right = 0.5 * (middle[0] + at(0, 1, 0))
        kept = 1.0 - jnp.maximum(right, 0.0) + jnp.minimum(left, 0.0)
        coef[1, x, low:high, :] = jnp.maximum(left, 0.0)
        coef[2, x, low:high, :] = -jnp.minimum(right, 0.0)
        left = 0.5 * (at(1, 0, -1) + middle[1])
        right = 0.5 * (middle[1] + at(1, 0, 1))
        kept = kept - jnp.maximum(right, 0.0) + jnp.minimum(left, 0.0)
        coef[3, x, low:high, :] = jnp.maximum(left, 0.0)
        coef[4, x, low:high, :] = -jnp.minimum(right, 0.0)
        before = jnp.where(lane == 0, 0.0, pltpu.roll(middle[2], 1, 1))
        after = jnp.where(lane == 127, 0.0, pltpu.roll(middle[2], 127, 1))
        left, right = 0.5 * (before + middle[2]), 0.5 * (middle[2] + after)
        kept = kept - jnp.maximum(right, 0.0) + jnp.minimum(left, 0.0)
        coef[5, x, low:high, :] = jnp.where(lane == 0, 0.0, jnp.maximum(left, 0.0))
        coef[6, x, low:high, :] = jnp.where(lane == 127, 0.0, -jnp.minimum(right, 0.0))
        coef[0, x, low:high, :] = kept
        return carry

    lax.fori_loop(1, SPAN - 1, coefficients, 0)

    groups = 32 // GROUP
    rates = [-rate[g * GROUP : (g + 1) * GROUP, :] for g in range(groups)]

    def row_of_step(step, reach, x, source, target, live):
        def cell(dx, y, g):
            return source[x + dx, y * 32 + g * GROUP : y * 32 + (g + 1) * GROUP, :]

        first, last = DEPTH - reach, DEPTH + 16 + reach
        before = [cell(0, first - 1, g) for g in range(groups)]
        now = [cell(0, first, g) for g in range(groups)]
        done = []
        for y in range(first, last):
            after = [cell(0, y + 1, g) for g in range(groups)]
            yv = y + ORIGIN - DEPTH
            k = [
                jnp.broadcast_to(coef[i, x, yv : yv + 1, :], (GROUP, 128)) for i in range(7)
            ]
            if step == 0:
                if y < DEPTH:
                    load = attach_low[x - 1, y - 1 : y, :]
                elif y < DEPTH + 16:
                    load = attach[x - 1, y - DEPTH : y - DEPTH + 1, :]
                else:
                    load = attach_high[x - 1, y - DEPTH - 16 : y - DEPTH - 15, :]
                kill = live
                if y < DEPTH:
                    kill = kill & ~edges[2]
                elif y >= DEPTH + 16:
                    kill = kill & ~edges[3]
                kill = kill.astype(jnp.float32)
            for g in range(groups):
                value = k[0] * now[g]
                value = value + k[1] * cell(-1, y, g)
                value = value + k[2] * cell(1, y, g)
                value = value + k[3] * before[g]
                value = value + k[4] * after[g]
                value = value + k[5] * pltpu.roll(now[g], 1, 1)
                value = value + k[6] * pltpu.roll(now[g], 127, 1)
                rows = slice(y * 32 + g * GROUP, y * 32 + (g + 1) * GROUP)
                if step == 0:
                    scale = jnp.exp(rates[g] * load) * kill
                    factor[x, rows, :] = scale
                else:
                    scale = factor[x, rows, :]
                value = value * scale
                if target is None:
                    done.append(value)
                else:
                    target[x, rows, :] = value
            before, now = now, after
        return done

    source, target = field, other
    for step in range(DEPTH):
        reach = DEPTH - 1 - step
        if step < DEPTH - 1:

            def middle_rows(i, carry, step=step, reach=reach, source=source, target=target):
                row_of_step(step, reach, DEPTH + i, source, target, jnp.bool_(True))
                return carry

            lax.fori_loop(0, 16, middle_rows, 0)
            for away in range(1, reach + 1):

                def outer(i, carry, away=away, step=step, reach=reach, source=source, target=target):
                    x = DEPTH - away + i * (15 + 2 * away)
                    live = jnp.where(i == 0, wide_at != 0, wide_at != wide_last)
                    row_of_step(step, reach - away, x, source, target, live)
                    return carry

                lax.fori_loop(0, 2, outer, 0)
        else:

            def last_rows(i, carry, step=step, source=source):
                done = row_of_step(step, 0, DEPTH + i, source, None, None)
                row = jnp.concatenate(done, axis=0).reshape(16, 32, 128)
                stage[:, i] = jnp.swapaxes(row, 0, 1)
                pltpu.make_async_copy(stage.at[:, i], out.at[:, i], out_sem).start()
                return carry

            lax.fori_loop(0, 16, last_rows, 0)
            pltpu.make_async_copy(stage, out, out_sem).wait()
        source, target = target, source


def transported(own, halos, velocity, attach, attach_low, attach_high, rate):
    vmem = pl.BlockSpec(memory_space=pltpu.VMEM)
    anywhere = pl.BlockSpec(memory_space=pl.ANY)
    return pl.pallas_call(
        transport_kernel,
        out_shape=jax.ShapeDtypeStruct((32, 16, 16, 128), jnp.float32),
        in_specs=[anywhere] * 10 + [vmem] * 4,
        out_specs=anywhere,
        scratch_shapes=[
            pltpu.VMEM((SPAN, SPAN * 32, 128), jnp.float32),
            pltpu.VMEM((SPAN, SPAN * 32, 128), jnp.float32),
            pltpu.VMEM((SPAN, SPAN * 32, 128), jnp.float32),
            pltpu.VMEM((3, SPAN, 32, 128), jnp.float32),
            pltpu.VMEM((7, SPAN, 32, 128), jnp.float32),
            pltpu.VMEM((2, 16, 16, 128), jnp.float32),
            pltpu.VMEM((4, CORNER_ROWS, 128), jnp.float32),
            pltpu.VMEM((32, 16, 16, 128), jnp.float32),
            pltpu.SemaphoreType.DMA((18,)),
            pltpu.SemaphoreType.DMA,
        ],
        compiler_params=params(),
    )(own, *halos, velocity, attach, attach_low, attach_high, rate)


def body(
    classes,
    velocity,
    attach_rate,
    bubble_pos,
    bubble_volume,
    bubble_area,
    bubble_count,
    cluster_target,
    cluster_offset,
):
    devices = lax.axis_size("wide") * lax.axis_size("narrow")
    meta = jnp.concatenate(
        [
            cluster_target.reshape(-1),
            bubble_count.reshape(-1),
            cluster_offset[:, 0],
            cluster_offset[:, 1],
        ]
    )
    sent = pack(meta, bubble_pos, bubble_volume, bubble_area, devices)
    got = lax.all_to_all(sent, AXES, split_axis=0, concat_axis=0, tiled=True)

    own, wide_low, wide_high, side_low, side_high, *corners = strips(classes, velocity)
    steps = ((1, 1), (1, -1), (-1, 1), (-1, -1))
    c00 = rolled(corners[3], *steps[0])
    c01 = rolled(corners[2], *steps[1])
    c10 = rolled(corners[1], *steps[2])
    c11 = rolled(corners[0], *steps[3])
    halos = (
        rolled(wide_high, 1, 0),
        rolled(wide_low, -1, 0),
        rolled(side_high, 0, 1),
        rolled(side_low, 0, -1),
        c00,
        c01,
        c10,
        c11,
    )
    deposit, attach = deposited(got)
    reach = DEPTH - 1
    tall = jnp.concatenate(
        [rolled(attach[-reach:], 1, 0), attach, rolled(attach[:reach], -1, 0)], axis=0
    )
    attach_low = rolled(tall[:, -reach:], 0, 1)
    attach_high = rolled(tall[:, :reach], 0, -1)
    rate = jnp.broadcast_to(attach_rate[:, None], (32, 128))
    return deposit, transported(
        own, halos, velocity, tall, attach_low, attach_high, rate
    )


def solution(mesh):
    return jax.shard_map(
        body,
        mesh=mesh,
        in_specs=(
            P(None, "wide", "narrow", None),
            P(None, "wide", "narrow", None),
            P(),
            P(("wide", "narrow"), None, None),
            P(("wide", "narrow"), None),
            P(("wide", "narrow"), None),
            P(("wide", "narrow"), None),
            P(("wide", "narrow"), None),
            P(("wide", "narrow"), None),
        ),
        out_specs=(P(None, "wide", "narrow", None), P(None, "wide", "narrow", None)),
        check_vma=False,
    )
```

```python
import functools

import jax
import jax.numpy as jnp
from jax import lax
from jax.experimental import pallas as pl
from jax.experimental.pallas import tpu as pltpu
from jax.sharding import PartitionSpec as P

WIN = 4
DEPTH = 4
GROUP = 8
AXES = ("wide", "narrow")
VMEM_BYTES = 60 * 1024 * 1024

CORNER = [(a, b) for a in range(DEPTH - 1) for b in range(DEPTH - 1 - a)]


def params(**more):
    return pltpu.CompilerParams(vmem_limit_bytes=VMEM_BYTES, **more)


def rolled(block, wide_step, narrow_step):
    wide_count, narrow_count = lax.axis_size("wide"), lax.axis_size("narrow")
    pairs = [
        (
            w * narrow_count + n,
            (w + wide_step) % wide_count * narrow_count + (n + narrow_step) % narrow_count,
        )
        for w in range(wide_count)
        for n in range(narrow_count)
    ]
    return lax.ppermute(block, AXES, pairs)


def pack_kernel(
    target_of, count_of, corner_of, pos, volume, area, classes, velocity,
    sent, wide_low, wide_high, side_low, side_high,
    tally, field, speed, sem,
):
    copies = []

    def copy(source, target):
        moved = pltpu.make_async_copy(source, target, sem.at[len(copies)])
        moved.start()
        copies.append(moved)

    copy(velocity, speed)
    for k in range(32):
        copy(classes.at[k], field.at[:, :, k])

    _, clusters, bubbles = pos.shape
    devices = sent.shape[0]
    row = count_of.shape[0]
    sent[...] = jnp.zeros_like(sent)

    def clear(d, carry):
        tally[d] = 0
        return carry

    lax.fori_loop(0, devices, clear, 0, unroll=8)
    lane = lax.broadcasted_iota(jnp.int32, (1, bubbles), 1)

    def some(r, carry):
        for i in range(row):
            c = r * row + i
            target, count = target_of[0, c], count_of[i, r]
            corner_x = corner_of[0, c].astype(jnp.float32)
            corner_y = corner_of[1, c].astype(jnp.float32)
            rank = tally[target]
            tally[target] = rank + 1
            live = lane < count
            at = pl.ds(c, 1)
            rows = [
                pos[0, at, :] * 4.0,
                pos[1, at, :] * 4.0,
                pos[2, at, :] * 128.0,
                jnp.where(live, volume[at, :], 0.0),
                jnp.where(live, area[at, :], 0.0),
            ]
            for j, value in enumerate(rows):
                start = pl.multiple_of((rank * 5 + j) * bubbles, bubbles)
                sent[target, :, pl.ds(start, bubbles)] = value
            tail = sent[target, :, pl.ds(10 * bubbles, bubbles)]
            tail = jnp.where(lane == 2 * rank, corner_x, tail)
            tail = jnp.where(lane == 2 * rank + 1, corner_y, tail)
            sent[target, :, pl.ds(10 * bubbles, bubbles)] = tail
        return carry

    lax.fori_loop(0, clusters // row, some, 0)

    for moved in copies:
        moved.wait()
    arrived = len(copies)
    for out, first in ((side_low, 0), (side_high, 16 - DEPTH)):
        copy(field.at[:, pl.ds(first, DEPTH)], out.at[:, pl.ds(0, DEPTH)])
        for d in range(3):
            rows = pl.ds(8 * d, 8)
            copy(speed.at[d, :, pl.ds(first // 8 * 8, 8)], out.at[:, DEPTH, rows])
    for out, first in ((wide_low, 0), (wide_high, 16 - DEPTH)):
        copy(field.at[pl.ds(first, DEPTH)], out.at[:, pl.ds(0, 16)])
        for d in range(3):
            rows = pl.ds(16 * d % 32, 16)
            copy(speed.at[d, pl.ds(first, DEPTH)], out.at[:, 16 + 16 * d // 32, rows])
    for moved in copies[arrived:]:
        moved.wait()


def pack(target_of, count_of, corner_of, pos, volume, area, classes, velocity, devices):
    bubbles = pos.shape[2]
    smem = pl.BlockSpec(memory_space=pltpu.SMEM)
    vmem = pl.BlockSpec(memory_space=pltpu.VMEM)
    anywhere = pl.BlockSpec(memory_space=pl.ANY)
    return pl.pallas_call(
        pack_kernel,
        out_shape=(jax.ShapeDtypeStruct((devices, 1, 11 * bubbles), jnp.float32),)
        + (jax.ShapeDtypeStruct((DEPTH, WIDE_CELLS, 32, 128), jnp.float32),) * 2
        + (jax.ShapeDtypeStruct((16, SIDE_CELLS, 32, 128), jnp.float32),) * 2,
        in_specs=[smem] * 3 + [vmem] * 3 + [anywhere] * 2,
        out_specs=(vmem,) + (anywhere,) * 4,
        scratch_shapes=[
            pltpu.SMEM((devices,), jnp.int32),
            pltpu.VMEM((16, 16, 32, 128), jnp.float32),
            pltpu.VMEM((3, 16, 16, 128), jnp.float32),
            pltpu.SemaphoreType.DMA((33 + 16,)),
        ],
        compiler_params=params(),
    )(target_of, count_of, corner_of, pos, volume, area, classes, velocity)


UNROLL = 16


def halves(value):
    high = value.astype(jnp.bfloat16)
    return high, (value - high.astype(jnp.float32)).astype(jnp.bfloat16)


def across(left, right):
    return lax.dot_general(
        left, right, (((1,), (1,)), ((), ())), preferred_element_type=jnp.float32
    )


def bell(distance):
    return jnp.exp2((distance * (-0.5 * 1.4426950408889634)) * distance)


def deposit_kernel(got_any, got, deposit, attach, total, corners, sem):
    devices = got.shape[0]
    bubbles = got.shape[2] // 11
    copy = pltpu.make_async_copy(
        got_any.at[:, :, pl.ds(10 * bubbles, bubbles)], corners, sem
    )
    copy.start()
    total[...] = jnp.zeros_like(total)
    copy.wait()
    row = lax.broadcasted_iota(jnp.int32, (8, bubbles), 0)
    is_volume = row % 2 == 0
    cell_y = (row // 2).astype(jnp.float32) + 0.5
    cell_z = lax.broadcasted_iota(jnp.int32, (128, bubbles), 0).astype(jnp.float32) + 0.5

    def sources(step, carry):
        done = []
        for u in range(UNROLL):
            for slot in range(2):
                source = step * UNROLL + u
                px, py, pz, vol, are = (
                    got[source, :, (5 * slot + i) * bubbles : (5 * slot + i + 1) * bubbles]
                    for i in range(5)
                )
                share = bell(cell_y - py) * jnp.where(is_volume, vol, are)
                plane = jnp.concatenate(
                    [share * bell((i + 0.5) - px) for i in range(WIN)], axis=0
                )
                plane_high, plane_low = halves(plane)
                high, low = halves(bell(cell_z - pz))
                left = jnp.concatenate(
                    [
                        jnp.concatenate([plane_high, plane_high], axis=1),
                        jnp.concatenate([plane_low, jnp.zeros_like(plane_low)], axis=1),
                    ],
                    axis=0,
                )
                both = across(left, jnp.concatenate([high, low], axis=1))
                window = both[:32] + both[32:]
                done.append((source, slot, window))
        for source, slot, window in done:
            x = corners[source, 0, 2 * slot].astype(jnp.int32)
            y = corners[source, 0, 2 * slot + 1].astype(jnp.int32)
            for i in range(WIN):
                at = pl.ds((x + i) * 32 + y * 2, 8)
                total[at, :] = total[at, :] + window[8 * i : 8 * i + 8]
        return carry

    lax.fori_loop(0, devices // UNROLL, sources, 0)
    for x in range(16):
        gas = total[pl.ds(x * 32, 16, stride=2), :]
        face = total[pl.ds(x * 32 + 1, 16, stride=2), :]
        deposit[0, x] = gas
        deposit[1, x] = face
        attach[x] = face / (1.0 + gas)


def deposited(got):
    devices = got.shape[0]
    return pl.pallas_call(
        deposit_kernel,
        out_shape=(
            jax.ShapeDtypeStruct((2, 16, 16, 128), jnp.float32),
            jax.ShapeDtypeStruct((16, 16, 128), jnp.float32),
        ),
        in_specs=[
            pl.BlockSpec(memory_space=pl.ANY),
            pl.BlockSpec(memory_space=pltpu.VMEM),
        ],
        out_specs=(pl.BlockSpec(memory_space=pltpu.VMEM),) * 2,
        scratch_shapes=[
            pltpu.VMEM((512, 128), jnp.float32),
            pltpu.SMEM((devices, 1, 128), jnp.float32),
            pltpu.SemaphoreType.DMA,
        ],
        compiler_params=params(),
    )(got, got)


WIDE_CELLS = 16 + 2
SIDE_CELLS = DEPTH + 1
CORNER_CELLS = len(CORNER) + DEPTH - 1


def corners_kernel(side_low, side_high, low, high, held, sem):
    reach = DEPTH - 1
    count = 0

    def run(pairs):
        nonlocal count
        moved = []
        for source, target in pairs:
            moved.append(pltpu.make_async_copy(source, target, sem.at[count]))
            moved[-1].start()
            count += 1
        for one in moved:
            one.wait()

    run(
        (block.at[pl.ds(first, reach)], held.at[at, side])
        for at, block in enumerate((side_low, side_high))
        for side, first in enumerate((0, 16 - reach))
    )
    pairs = []
    for side, out in enumerate((low, high)):
        for at in range(2):
            cell = 0
            for a in range(reach):
                x, cells = reach - 1 - a if side else a, reach - a
                first = 0 if at else DEPTH - cells
                block = held.at[at, side, x]
                pairs.append((block.at[pl.ds(first, cells)], out.at[at, pl.ds(cell, cells)]))
                cell += cells
                pairs.append((block.at[DEPTH], out.at[at, len(CORNER) + a]))
    run(pairs)


def corners_of(side_low, side_high):
    anywhere = pl.BlockSpec(memory_space=pl.ANY)
    reach = DEPTH - 1
    return pl.pallas_call(
        corners_kernel,
        out_shape=(jax.ShapeDtypeStruct((2, CORNER_CELLS, 32, 128), jnp.float32),) * 2,
        in_specs=[anywhere] * 2,
        out_specs=(anywhere,) * 2,
        scratch_shapes=[
            pltpu.VMEM((2, 2, reach, SIDE_CELLS, 32, 128), jnp.float32),
            pltpu.SemaphoreType.DMA((4 + 8 * reach,)),
        ],
        compiler_params=params(),
    )(side_low, side_high)


SPAN = 16 + 2 * DEPTH
BLOCK = 2
PART = 4
ORIGIN = 8


def transport_kernel(
    classes, velocity, wide_low, wide_high, side_low, side_high, corner_low, corner_high,
    rate, attach, beside_low, beside_high, above_low, above_high,
    out,
    field, other, factor, speed, coef, load, sem, out_sem,
):
    copies = []

    def copy(source, target):
        moved = pltpu.make_async_copy(source, target, sem.at[len(copies)])
        moved.start()
        copies.append(moved)

    inner = pl.ds(DEPTH, 16)
    copy(velocity, speed.at[:, inner, pl.ds(ORIGIN, 16)])
    for block, first in ((wide_low, 0), (wide_high, 16 + DEPTH)):
        for d in range(3):
            copy(
                block.at[:, 16 + 16 * d // 32, pl.ds(16 * d % 32, 16)],
                speed.at[d, pl.ds(first, DEPTH), pl.ds(ORIGIN, 16)],
            )
    for block, first in ((side_low, 0), (side_high, ORIGIN + 16)):
        for d in range(3):
            copy(block.at[:, DEPTH, pl.ds(8 * d, 8)], speed.at[d, inner, pl.ds(first, 8)])
    turns = ((corner_low, False), (corner_high, True))
    for block, is_high in turns:
        for at, first in enumerate((0, ORIGIN + 16)):
            for a in range(DEPTH - 1):
                x = 16 + DEPTH + a if is_high else DEPTH - 1 - a
                for d in range(3):
                    copy(
                        block.at[at, len(CORNER) + a, pl.ds(8 * d, 8)],
                        speed.at[d, x, pl.ds(first, 8)],
                    )
    speeds = len(copies)
    for k in range(32):
        copy(classes.at[k], field.at[inner, inner, k])
    for block, first in ((wide_low, 0), (wide_high, 16 + DEPTH)):
        copy(block.at[:, pl.ds(0, 16)], field.at[pl.ds(first, DEPTH), inner])
    for block, first in ((side_low, 0), (side_high, 16 + DEPTH)):
        copy(block.at[:, pl.ds(0, DEPTH)], field.at[inner, pl.ds(first, DEPTH)])
    for block, is_high in turns:
        for at, first in enumerate((0, 16 + DEPTH)):
            cell = 0
            for a in range(DEPTH - 1):
                x = 16 + DEPTH + a if is_high else DEPTH - 1 - a
                run = DEPTH - 1 - a
                y = first if at else DEPTH - run
                copy(block.at[at, pl.ds(cell, run)], field.at[x, pl.ds(y, run)])
                cell += run
    for moved in copies[:speeds]:
        moved.wait()

    wide_at, narrow_at = lax.axis_index("wide"), lax.axis_index("narrow")
    wide_last, narrow_last = lax.axis_size("wide") - 1, lax.axis_size("narrow") - 1
    edges = (wide_at == 0, wide_at == wide_last, narrow_at == 0, narrow_at == narrow_last)
    spans = ((0, DEPTH), (16 + DEPTH, SPAN))

    for side, (first, last) in enumerate(spans):

        @pl.when(edges[side])
        def _(first=first, last=last):
            speed[:, first:last] = jnp.zeros((3, last - first) + speed.shape[2:], jnp.float32)

        @pl.when(edges[2 + side])
        def _(first=first, last=last):
            shift = ORIGIN - DEPTH
            speed[:, :, first + shift : last + shift] = jnp.zeros(
                (3, SPAN, last - first, 128), jnp.float32
            )

    lane = lax.broadcasted_iota(jnp.int32, (SPAN - 2, 128), 1)

    def coefficients(x, carry):
        low, high = ORIGIN - DEPTH + 1, ORIGIN + 16 + DEPTH - 1

        def at(d, dx, dy):
            return speed[d, x + dx, low + dy : high + dy, :]

        middle = [at(d, 0, 0) for d in range(3)]
        left = 0.5 * (at(0, -1, 0) + middle[0])
        right = 0.5 * (middle[0] + at(0, 1, 0))
        kept = 1.0 - jnp.maximum(right, 0.0) + jnp.minimum(left, 0.0)
        coef[1, x, low:high, :] = jnp.maximum(left, 0.0)
        coef[2, x, low:high, :] = -jnp.minimum(right, 0.0)
        left = 0.5 * (at(1, 0, -1) + middle[1])
        right = 0.5 * (middle[1] + at(1, 0, 1))
        kept = kept - jnp.maximum(right, 0.0) + jnp.minimum(left, 0.0)
        coef[3, x, low:high, :] = jnp.maximum(left, 0.0)
        coef[4, x, low:high, :] = -jnp.minimum(right, 0.0)
        before = jnp.where(lane == 0, 0.0, pltpu.roll(middle[2], 1, 1))
        after = jnp.where(lane == 127, 0.0, pltpu.roll(middle[2], 127, 1))
        left, right = 0.5 * (before + middle[2]), 0.5 * (middle[2] + after)
        kept = kept - jnp.maximum(right, 0.0) + jnp.minimum(left, 0.0)
        coef[5, x, low:high, :] = jnp.where(lane == 0, 0.0, jnp.maximum(left, 0.0))
        coef[6, x, low:high, :] = jnp.where(lane == 127, 0.0, -jnp.minimum(right, 0.0))
        coef[0, x, low:high, :] = kept
        return carry

    lax.fori_loop(1, SPAN - 1, coefficients, 0)
    for moved in copies[speeds:]:
        moved.wait()
    for side, (first, last) in enumerate(spans):

        @pl.when(edges[side])
        def _(first=first, last=last):
            field[first:last] = jnp.zeros((last - first, SPAN, 32, 128), jnp.float32)

        @pl.when(edges[2 + side])
        def _(first=first, last=last):
            field[:, first:last] = jnp.zeros((SPAN, last - first, 32, 128), jnp.float32)


    groups = 32 // GROUP
    at_class = lax.broadcasted_iota(jnp.int32, (GROUP, 128), 0)
    rates = []
    for g in range(groups):
        value = jnp.zeros((GROUP, 128), jnp.float32)
        for i in range(GROUP):
            value = jnp.where(at_class == i, -rate[g * GROUP + i], value)
        rates.append(value)
    reach = DEPTH - 1
    load[1:DEPTH, 1 : SPAN - 1, :] = above_low[...]
    load[DEPTH + 16 : SPAN - 1, 1 : SPAN - 1, :] = above_high[...]
    load[DEPTH : DEPTH + 16, 1:DEPTH, :] = beside_low[...]
    load[DEPTH : DEPTH + 16, DEPTH : DEPTH + 16, :] = attach[...]
    load[DEPTH : DEPTH + 16, DEPTH + 16 : SPAN - 1, :] = beside_high[...]

    def row_of_step(step, reach, x, source, target, live):
        def cell(dx, y, g):
            return source[x + dx, y, g * GROUP : (g + 1) * GROUP, :]

        first, last = DEPTH - reach, DEPTH + 16 + reach
        before = [cell(0, first - 1, g) for g in range(groups)]
        now = [cell(0, first, g) for g in range(groups)]
        done = []
        for y in range(first, last):
            after = [cell(0, y + 1, g) for g in range(groups)]
            yv = y + ORIGIN - DEPTH
            k = [
                jnp.broadcast_to(coef[i, x, yv : yv + 1, :], (GROUP, 128)) for i in range(7)
            ]
            if step == 0:
                kill = live
                if y < DEPTH:
                    kill = kill & ~edges[2]
                elif y >= DEPTH + 16:
                    kill = kill & ~edges[3]
                kill = kill.astype(jnp.float32)
                loaded = load[x, y : y + 1, :]
            for g in range(groups):
                value = k[0] * now[g]
                value = value + k[1] * cell(-1, y, g)
                value = value + k[2] * cell(1, y, g)
                value = value + k[3] * before[g]
                value = value + k[4] * after[g]
                value = value + k[5] * pltpu.roll(now[g], 1, 1)
                value = value + k[6] * pltpu.roll(now[g], 127, 1)
                at = (x, y, slice(g * GROUP, (g + 1) * GROUP))
                if step == 0:
                    scale = jnp.exp(rates[g] * loaded) * kill
                    done.append((factor, at, scale))
                else:
                    scale = factor[at]
                done.append((target, at, value * scale))
            before, now = now, after
            if (y - first) % BLOCK == BLOCK - 1 or y == last - 1:
                for ref, at, value in done:
                    ref[at] = value
                done = []

    source, target = field, other
    for step in range(DEPTH):
        reach = DEPTH - 1 - step

        def middle_rows(i, carry, step=step, reach=reach, source=source, target=target):
            x = DEPTH + 2 * i
            live = jnp.bool_(True)
            row_of_step(step, reach, x, source, target, live)
            row_of_step(step, reach, x + 1, source, target, live)
            return carry

        if step < DEPTH - 1:
            lax.fori_loop(0, 8, middle_rows, 0)
        else:
            for part in range(0, 16, PART):
                lax.fori_loop(part // 2, (part + PART) // 2, middle_rows, 0)
                for k in range(32):
                    pltpu.make_async_copy(
                        target.at[pl.ds(DEPTH + part, PART), inner, k],
                        out.at[k, pl.ds(part, PART)],
                        out_sem,
                    ).start()
        for away in range(1, reach + 1):

            def outer(i, carry, away=away, step=step, reach=reach, source=source, target=target):
                x = DEPTH - away + i * (15 + 2 * away)
                live = jnp.where(i == 0, wide_at != 0, wide_at != wide_last)
                row_of_step(step, reach - away, x, source, target, live)
                return carry

            lax.fori_loop(0, 2, outer, 0)
        source, target = target, source
    pltpu.make_async_copy(out, out, out_sem).wait()


def transported(classes, velocity, halos, rate, *attach):
    vmem = pl.BlockSpec(memory_space=pltpu.VMEM)
    anywhere = pl.BlockSpec(memory_space=pl.ANY)
    return pl.pallas_call(
        transport_kernel,
        out_shape=jax.ShapeDtypeStruct((32, 16, 16, 128), jnp.float32),
        in_specs=[anywhere] * 8 + [pl.BlockSpec(memory_space=pltpu.SMEM)] + [vmem] * 5,
        out_specs=anywhere,
        scratch_shapes=[
            pltpu.VMEM((SPAN, SPAN, 32, 128), jnp.float32),
            pltpu.VMEM((SPAN, SPAN, 32, 128), jnp.float32),
            pltpu.VMEM((SPAN, SPAN, 32, 128), jnp.float32),
            pltpu.VMEM((3, SPAN, 32, 128), jnp.float32),
            pltpu.VMEM((7, SPAN, 32, 128), jnp.float32),
            pltpu.VMEM((SPAN, SPAN, 128), jnp.float32),
            pltpu.SemaphoreType.DMA((97,)),
            pltpu.SemaphoreType.DMA,
        ],
        compiler_params=params(),
    )(classes, velocity, *halos, rate, *attach)


def body(
    classes,
    velocity,
    attach_rate,
    bubble_pos,
    bubble_volume,
    bubble_area,
    bubble_count,
    cluster_target,
    cluster_offset,
):
    devices = lax.axis_size("wide") * lax.axis_size("narrow")
    sent, out_low, out_high, aside_low, aside_high = pack(
        cluster_target.T,
        bubble_count.T,
        cluster_offset.T,
        jnp.transpose(bubble_pos, (1, 0, 2)),
        bubble_volume,
        bubble_area,
        classes,
        velocity,
        devices,
    )
    got = lax.all_to_all(sent, AXES, split_axis=0, concat_axis=0, tiled=True)

    side_low, side_high = rolled(aside_high, 0, 1), rolled(aside_low, 0, -1)
    turn_low, turn_high = corners_of(side_low, side_high)
    got, turn_low, turn_high, out_low, out_high = lax.optimization_barrier(
        (got, turn_low, turn_high, out_low, out_high)
    )
    wide_low, wide_high = rolled(out_high, 1, 0), rolled(out_low, -1, 0)
    corner_low, corner_high = rolled(turn_high, 1, 0), rolled(turn_low, -1, 0)
    deposit, attach = deposited(got)
    reach = DEPTH - 1
    beside_low = rolled(attach[:, -reach:], 0, 1)
    beside_high = rolled(attach[:, :reach], 0, -1)

    def across_sides(rows):
        return jnp.concatenate([beside_low[rows], attach[rows], beside_high[rows]], axis=1)

    last = across_sides(slice(-reach, None))
    first = across_sides(slice(0, reach))
    above_low, above_high = rolled(last, 1, 0), rolled(first, -1, 0)
    halos = (wide_low, wide_high, side_low, side_high, corner_low, corner_high)
    return deposit, transported(
        classes, velocity, halos, attach_rate,
        attach, beside_low, beside_high, above_low, above_high,
    )


def solution(mesh):
    return jax.shard_map(
        body,
        mesh=mesh,
        in_specs=(
            P(None, "wide", "narrow", None),
            P(None, "wide", "narrow", None),
            P(),
            P(("wide", "narrow"), None, None),
            P(("wide", "narrow"), None),
            P(("wide", "narrow"), None),
            P(("wide", "narrow"), None),
            P(("wide", "narrow"), None),
            P(("wide", "narrow"), None),
        ),
        out_specs=(P(None, "wide", "narrow", None), P(None, "wide", "narrow", None)),
        check_vma=False,
    )
```

```python
import functools

import jax
import jax.numpy as jnp
from jax import lax
from jax.experimental import pallas as pl
from jax.experimental.pallas import tpu as pltpu
from jax.sharding import PartitionSpec as P

WIN = 4
DEPTH = 4
REACH = DEPTH - 1
GROUP = 8
AXES = ("wide", "narrow")
VMEM_BYTES = 60 * 1024 * 1024

CORNER = [(a, b) for a in range(REACH - 1) for b in range(REACH - 1 - a)]


def params(**more):
    return pltpu.CompilerParams(vmem_limit_bytes=VMEM_BYTES, **more)


def rolled(block, wide_step, narrow_step):
    wide_count, narrow_count = lax.axis_size("wide"), lax.axis_size("narrow")
    pairs = [
        (
            w * narrow_count + n,
            (w + wide_step) % wide_count * narrow_count + (n + narrow_step) % narrow_count,
        )
        for w in range(wide_count)
        for n in range(narrow_count)
    ]
    return lax.ppermute(block, AXES, pairs)


def wide_speed(i, d):
    return 16 + 2 * i + d // 2, pl.ds(16 * (d % 2), 16)


def edges_kernel(
    classes, velocity, wide_low, wide_high, side_low, side_high, field, speed, sem
):
    copies = []

    def copy(source, target):
        moved = pltpu.make_async_copy(source, target, sem.at[len(copies)])
        moved.start()
        copies.append(moved)

    copy(velocity, speed)
    for x, row in ((0, 0), (15, 1)):
        for k in range(32):
            copy(classes.at[k, x], field.at[row, :, k])
    aside = len(copies)
    for first in (0, 1):
        for k in range(32):
            copy(classes.at[k, :, pl.ds(8 * first, 8)], field.at[pl.ds(2, 16), pl.ds(8 * first, 8), k])
    for moved in copies[:aside]:
        moved.wait()
    leaving = len(copies)
    for out, row, first in ((wide_low, 0, 0), (wide_high, 1, 16 - REACH)):
        copy(field.at[row], out.at[pl.ds(0, 16)])
        for i in range(REACH):
            for d in range(3):
                copy(speed.at[d, first + i], out.at[wide_speed(i, d)])
    for out, y in ((side_low, 0), (side_high, 15)):
        for d in range(3):
            copy(speed.at[d, :, pl.ds(y // 8 * 8, 8)], out.at[:, 1, pl.ds(8 * d, 8)])
    for moved in copies[aside:leaving]:
        moved.wait()
    for out, y in ((side_low, 0), (side_high, 15)):
        copy(field.at[pl.ds(2, 16), y], out.at[:, 0])
    for moved in copies[leaving:]:
        moved.wait()


def edges_of(classes, velocity):
    anywhere = pl.BlockSpec(memory_space=pl.ANY)
    return pl.pallas_call(
        edges_kernel,
        out_shape=(jax.ShapeDtypeStruct((16 + 2 * REACH, 32, 128), jnp.float32),) * 2
        + (jax.ShapeDtypeStruct((16, 2, 32, 128), jnp.float32),) * 2,
        in_specs=[anywhere] * 2,
        out_specs=(anywhere,) * 4,
        scratch_shapes=[
            pltpu.VMEM((18, 16, 32, 128), jnp.float32),
            pltpu.VMEM((3, 16, 16, 128), jnp.float32),
            pltpu.SemaphoreType.DMA((129 + 8 + 2 + 6 * REACH,)),
        ],
        compiler_params=params(),
    )(classes, velocity)


def pack_kernel(target_of, count_of, corner_of, pos, volume, area, sent, tally):
    _, clusters, bubbles = pos.shape
    devices = sent.shape[0]
    row = count_of.shape[0]
    sent[...] = jnp.zeros_like(sent)

    def clear(d, carry):
        tally[d] = 0
        return carry

    lax.fori_loop(0, devices, clear, 0, unroll=8)
    lane = lax.broadcasted_iota(jnp.int32, (1, bubbles), 1)

    def some(r, carry):
        for i in range(row):
            c = r * row + i
            target, count = target_of[0, c], count_of[i, r]
            corner_x = corner_of[0, c].astype(jnp.float32)
            corner_y = corner_of[1, c].astype(jnp.float32)
            rank = tally[target]
            tally[target] = rank + 1
            live = lane < count
            at = pl.ds(c, 1)
            rows = [
                pos[0, at, :] * 4.0,
                pos[1, at, :] * 4.0,
                pos[2, at, :] * 128.0,
                jnp.where(live, volume[at, :], 0.0),
                jnp.where(live, area[at, :], 0.0),
            ]
            for j, value in enumerate(rows):
                start = pl.multiple_of((rank * 5 + j) * bubbles, bubbles)
                sent[target, :, pl.ds(start, bubbles)] = value
            tail = sent[target, :, pl.ds(10 * bubbles, bubbles)]
            tail = jnp.where(lane == 2 * rank, corner_x, tail)
            tail = jnp.where(lane == 2 * rank + 1, corner_y, tail)
            sent[target, :, pl.ds(10 * bubbles, bubbles)] = tail
        return carry

    lax.fori_loop(0, clusters // row, some, 0)


def pack(target_of, count_of, corner_of, pos, volume, area, devices):
    bubbles = pos.shape[2]
    return pl.pallas_call(
        pack_kernel,
        out_shape=jax.ShapeDtypeStruct((devices, 1, 11 * bubbles), jnp.float32),
        in_specs=[pl.BlockSpec(memory_space=pltpu.SMEM)] * 3
        + [pl.BlockSpec(memory_space=pltpu.VMEM)] * 3,
        out_specs=pl.BlockSpec(memory_space=pltpu.VMEM),
        scratch_shapes=[pltpu.SMEM((devices,), jnp.int32)],
        compiler_params=params(),
    )(target_of, count_of, corner_of, pos, volume, area)


UNROLL = 32


def halves(value):
    high = value.astype(jnp.bfloat16)
    return high, (value - high.astype(jnp.float32)).astype(jnp.bfloat16)


def across(left, right):
    return lax.dot_general(
        left, right, (((1,), (1,)), ((), ())), preferred_element_type=jnp.float32
    )


def bell(distance):
    return jnp.exp2((distance * (-0.5 * 1.4426950408889634)) * distance)


def deposit_kernel(got_any, got, deposit, attach, total, corners, sem):
    devices = got.shape[0]
    bubbles = got.shape[2] // 11
    copy = pltpu.make_async_copy(
        got_any.at[:, :, pl.ds(10 * bubbles, bubbles)], corners, sem
    )
    copy.start()
    total[...] = jnp.zeros_like(total)
    copy.wait()
    row = lax.broadcasted_iota(jnp.int32, (8, bubbles), 0)
    is_volume = row % 2 == 0
    cell_y = (row // 2).astype(jnp.float32) + 0.5
    cell_z = lax.broadcasted_iota(jnp.int32, (128, bubbles), 0).astype(jnp.float32) + 0.5

    def sources(step, carry):
        done = []
        for u in range(UNROLL):
            for slot in range(2):
                source = step * UNROLL + u
                px, py, pz, vol, are = (
                    got[source, :, (5 * slot + i) * bubbles : (5 * slot + i + 1) * bubbles]
                    for i in range(5)
                )
                share = bell(cell_y - py) * jnp.where(is_volume, vol, are)
                plane = jnp.concatenate(
                    [share * bell((i + 0.5) - px) for i in range(WIN)], axis=0
                )
                plane_high, plane_low = halves(plane)
                high, low = halves(bell(cell_z - pz))
                left = jnp.concatenate(
                    [
                        jnp.concatenate([plane_high, plane_high], axis=1),
                        jnp.concatenate([plane_low, jnp.zeros_like(plane_low)], axis=1),
                    ],
                    axis=0,
                )
                both = across(left, jnp.concatenate([high, low], axis=1))
                window = both[:32] + both[32:]
                done.append((source, slot, window))
        for source, slot, window in done:
            x = corners[source, 0, 2 * slot].astype(jnp.int32)
            y = corners[source, 0, 2 * slot + 1].astype(jnp.int32)
            for i in range(WIN):
                at = pl.ds((x + i) * 32 + y * 2, 8)
                total[at, :] = total[at, :] + window[8 * i : 8 * i + 8]
        return carry

    lax.fori_loop(0, devices // UNROLL, sources, 0)
    for x in range(16):
        gas = total[pl.ds(x * 32, 16, stride=2), :]
        face = total[pl.ds(x * 32 + 1, 16, stride=2), :]
        deposit[0, x] = gas
        deposit[1, x] = face
        attach[x] = face / (1.0 + gas)


def deposited(got):
    devices = got.shape[0]
    return pl.pallas_call(
        deposit_kernel,
        out_shape=(
            jax.ShapeDtypeStruct((2, 16, 16, 128), jnp.float32),
            jax.ShapeDtypeStruct((16, 16, 128), jnp.float32),
        ),
        in_specs=[
            pl.BlockSpec(memory_space=pl.ANY),
            pl.BlockSpec(memory_space=pltpu.VMEM),
        ],
        out_specs=(pl.BlockSpec(memory_space=pltpu.VMEM),) * 2,
        scratch_shapes=[
            pltpu.VMEM((512, 128), jnp.float32),
            pltpu.SMEM((devices, 1, 128), jnp.float32),
            pltpu.SemaphoreType.DMA,
        ],
        compiler_params=params(),
    )(got, got)


SPAN = 16 + 2 * DEPTH
ORIGIN = 8
BLOCK = 2
PART = 4
GROUPS = 32 // GROUP


def fill_coefficients(speed, coef, x, low, high):
    lane = lax.broadcasted_iota(jnp.int32, (high - low, 128), 1)

    def at(d, dx, dy):
        return speed[d, x + dx, low + dy : high + dy, :]

    middle = [at(d, 0, 0) for d in range(3)]
    left = 0.5 * (at(0, -1, 0) + middle[0])
    right = 0.5 * (middle[0] + at(0, 1, 0))
    kept = 1.0 - jnp.maximum(right, 0.0) + jnp.minimum(left, 0.0)
    coef[1, x, low:high, :] = jnp.maximum(left, 0.0)
    coef[2, x, low:high, :] = -jnp.minimum(right, 0.0)
    left = 0.5 * (at(1, 0, -1) + middle[1])
    right = 0.5 * (middle[1] + at(1, 0, 1))
    kept = kept - jnp.maximum(right, 0.0) + jnp.minimum(left, 0.0)
    coef[3, x, low:high, :] = jnp.maximum(left, 0.0)
    coef[4, x, low:high, :] = -jnp.minimum(right, 0.0)
    before = jnp.where(lane == 0, 0.0, pltpu.roll(middle[2], 1, 1))
    after = jnp.where(lane == 127, 0.0, pltpu.roll(middle[2], 127, 1))
    left, right = 0.5 * (before + middle[2]), 0.5 * (middle[2] + after)
    kept = kept - jnp.maximum(right, 0.0) + jnp.minimum(left, 0.0)
    coef[5, x, low:high, :] = jnp.where(lane == 0, 0.0, jnp.maximum(left, 0.0))
    coef[6, x, low:high, :] = jnp.where(lane == 127, 0.0, -jnp.minimum(right, 0.0))
    coef[0, x, low:high, :] = kept


def move_row(source, coef, x, first, last, to_speed, finish):
    def cell(dx, y, g):
        return source[x + dx, y, g * GROUP : (g + 1) * GROUP, :]

    before = [cell(0, first - 1, g) for g in range(GROUPS)]
    now = [cell(0, first, g) for g in range(GROUPS)]
    done = []
    for y in range(first, last):
        after = [cell(0, y + 1, g) for g in range(GROUPS)]
        yv = y + to_speed
        k = [jnp.broadcast_to(coef[i, x, yv : yv + 1, :], (GROUP, 128)) for i in range(7)]
        for g in range(GROUPS):
            value = k[0] * now[g]
            value = value + k[1] * cell(-1, y, g)
            value = value + k[2] * cell(1, y, g)
            value = value + k[3] * before[g]
            value = value + k[4] * after[g]
            value = value + k[5] * pltpu.roll(now[g], 1, 1)
            value = value + k[6] * pltpu.roll(now[g], 127, 1)
            done.append(finish((x, y, slice(g * GROUP, (g + 1) * GROUP)), value))
        before, now = now, after
        if (y - first) % BLOCK == BLOCK - 1 or y == last - 1:
            for ref, at, value in done:
                ref[at] = value
            done = []


def brick_edges():
    wide_at, narrow_at = lax.axis_index("wide"), lax.axis_index("narrow")
    wide_last, narrow_last = lax.axis_size("wide") - 1, lax.axis_size("narrow") - 1
    return wide_at == 0, wide_at == wide_last, narrow_at == 0, narrow_at == narrow_last


def first_kernel(
    classes, velocity, wide_low, wide_high, side_low, side_high,
    own, out_low, out_high, aside_low, aside_high,
    field, moved, speed, coef, sem,
):
    copies = []

    def copy(source, target):
        one = pltpu.make_async_copy(source, target, sem.at[len(copies)])
        one.start()
        copies.append(one)

    inner = pl.ds(1, 16)
    copy(velocity, speed.at[:, inner, pl.ds(ORIGIN, 16)])
    for d in range(3):
        copy(wide_low.at[wide_speed(REACH - 1, d)], speed.at[d, 0, pl.ds(ORIGIN, 16)])
        copy(wide_high.at[wide_speed(0, d)], speed.at[d, 17, pl.ds(ORIGIN, 16)])
        copy(side_low.at[:, 1, pl.ds(8 * d, 8)], speed.at[d, inner, pl.ds(0, 8)])
        copy(side_high.at[:, 1, pl.ds(8 * d, 8)], speed.at[d, inner, pl.ds(ORIGIN + 16, 8)])
    speeds = len(copies)
    for k in range(32):
        copy(classes.at[k], field.at[inner, inner, k])
    copy(wide_low.at[pl.ds(0, 16)], field.at[0, inner])
    copy(wide_high.at[pl.ds(0, 16)], field.at[17, inner])
    copy(side_low.at[:, 0], field.at[inner, 0])
    copy(side_high.at[:, 0], field.at[inner, 17])
    for one in copies[:speeds]:
        one.wait()
    edges = brick_edges()
    row = jnp.zeros((18, 32, 128), jnp.float32)
    for at, x in ((0, 0), (1, 17)):

        @pl.when(edges[at])
        def _(x=x):
            for d in range(3):
                speed[d, x] = jnp.zeros((32, 128), jnp.float32)

    for at, y in ((2, 0), (3, ORIGIN + 16)):

        @pl.when(edges[at])
        def _(y=y):
            speed[:, :, y : y + 8] = jnp.zeros((3, 18, 8, 128), jnp.float32)

    def coefficients(x, carry):
        fill_coefficients(speed, coef, x, ORIGIN, ORIGIN + 16)
        return carry

    lax.fori_loop(1, 17, coefficients, 0)
    for one in copies[speeds:]:
        one.wait()
    for at, here in ((0, 0), (1, 17)):

        @pl.when(edges[at])
        def _(here=here):
            field[here] = row

        @pl.when(edges[2 + at])
        def _(here=here):
            field[:, here] = row

    def rows(i, carry):
        for x in (1 + 2 * i, 2 + 2 * i):

            def finish(at, value):
                return moved, (at[0] - 1, at[1] - 1, at[2]), value

            move_row(field, coef, x, 1, 17, ORIGIN - 1, finish)
        return carry

    lax.fori_loop(0, 8, rows, 0)
    started = len(copies)
    copy(moved.at[pl.ds(0, REACH)], out_low)
    copy(moved.at[pl.ds(16 - REACH, REACH)], out_high)
    copy(moved.at[:, pl.ds(0, REACH)], aside_low)
    copy(moved.at[:, pl.ds(16 - REACH, REACH)], aside_high)
    copy(moved, own)
    for one in copies[started:]:
        one.wait()


def first_moved(classes, velocity, *halos):
    anywhere = pl.BlockSpec(memory_space=pl.ANY)
    return pl.pallas_call(
        first_kernel,
        out_shape=(jax.ShapeDtypeStruct((16, 16, 32, 128), jnp.float32),)
        + (jax.ShapeDtypeStruct((REACH, 16, 32, 128), jnp.float32),) * 2
        + (jax.ShapeDtypeStruct((16, REACH, 32, 128), jnp.float32),) * 2,
        in_specs=[anywhere] * 6,
        out_specs=(anywhere,) * 5,
        scratch_shapes=[
            pltpu.VMEM((18, 18, 32, 128), jnp.float32),
            pltpu.VMEM((16, 16, 32, 128), jnp.float32),
            pltpu.VMEM((3, 18, 32, 128), jnp.float32),
            pltpu.VMEM((7, 18, 32, 128), jnp.float32),
            pltpu.SemaphoreType.DMA((13 + 36 + 5,)),
        ],
        compiler_params=params(),
    )(classes, velocity, *halos)


TURN = len(CORNER) + REACH - 1
TURN_CELLS = 2 * TURN + REACH


def turns_kernel(
    aside_low, aside_high, side_low, side_high, attach, beside_low, beside_high, low, high, sem
):
    copies = []
    for side, out in enumerate((low, high)):
        for at, (block, speeds) in enumerate(((aside_low, side_low), (aside_high, side_high))):
            cell = TURN * at
            for a in range(REACH - 1):
                x, cells = 15 - a if side else a, REACH - 1 - a
                first = 0 if at else REACH - cells
                copies.append((block.at[x, pl.ds(first, cells)], out.at[pl.ds(cell, cells)]))
                cell += cells
                copies.append((speeds.at[x, 1], out.at[TURN * at + len(CORNER) + a]))
    moved = [
        pltpu.make_async_copy(source, target, sem.at[i])
        for i, (source, target) in enumerate(copies)
    ]
    for one in moved:
        one.start()
    for first, out in ((0, low), (16 - REACH, high)):
        for i in range(REACH):
            out[2 * TURN + i, 0:REACH, :] = beside_low[first + i]
            out[2 * TURN + i, REACH : REACH + 16, :] = attach[first + i]
            out[2 * TURN + i, REACH + 16 : 2 * REACH + 16, :] = beside_high[first + i]
    for one in moved:
        one.wait()


def turns(*operands):
    anywhere = pl.BlockSpec(memory_space=pl.ANY)
    vmem = pl.BlockSpec(memory_space=pltpu.VMEM)
    return pl.pallas_call(
        turns_kernel,
        out_shape=(jax.ShapeDtypeStruct((TURN_CELLS, 32, 128), jnp.float32),) * 2,
        in_specs=[anywhere] * 4 + [vmem] * 3,
        out_specs=(vmem,) * 2,
        scratch_shapes=[pltpu.SemaphoreType.DMA((8 * (REACH - 1),))],
        compiler_params=params(),
    )(*operands)


def transport_kernel(
    own, velocity, out_low, out_high, aside_low, aside_high,
    wide_low, wide_high, side_low, side_high, turn_low, turn_high,
    rate, attach, beside_low, beside_high,
    out,
    field, other, factor, speed, coef, load, above, sem, out_sem,
):
    copies = []

    def copy(source, target):
        moved = pltpu.make_async_copy(source, target, sem.at[len(copies)])
        moved.start()
        copies.append(moved)

    inner = pl.ds(DEPTH, 16)
    copy(velocity, speed.at[:, inner, pl.ds(ORIGIN, 16)])
    for block, first in ((wide_low, DEPTH - REACH), (wide_high, 16 + DEPTH)):
        for i in range(REACH):
            for d in range(3):
                copy(
                    block.at[wide_speed(i, d)],
                    speed.at[d, first + i, pl.ds(ORIGIN, 16)],
                )
    for block, first in ((side_low, 0), (side_high, ORIGIN + 16)):
        for d in range(3):
            copy(block.at[:, 1, pl.ds(8 * d, 8)], speed.at[d, inner, pl.ds(first, 8)])
    for side, block in enumerate((turn_low, turn_high)):
        copy(block.at[pl.ds(2 * TURN, REACH)], above.at[side])
        for at, first in enumerate((0, ORIGIN + 16)):
            for a in range(REACH - 1):
                x = 16 + DEPTH + a if side else DEPTH - 1 - a
                for d in range(3):
                    copy(
                        block.at[TURN * at + len(CORNER) + a, pl.ds(8 * d, 8)],
                        speed.at[d, x, pl.ds(first, 8)],
                    )
    speeds = len(copies)
    copy(own, field.at[inner, inner])
    for block, first in ((out_low, DEPTH - REACH), (out_high, 16 + DEPTH)):
        copy(block, field.at[pl.ds(first, REACH), inner])
    for block, first in ((aside_low, DEPTH - REACH), (aside_high, 16 + DEPTH)):
        copy(block, field.at[inner, pl.ds(first, REACH)])
    for side, block in enumerate((turn_low, turn_high)):
        for at in range(2):
            cell = TURN * at
            for a in range(REACH - 1):
                x = 16 + DEPTH + a if side else DEPTH - 1 - a
                run = REACH - 1 - a
                y = 16 + DEPTH if at else DEPTH - run
                copy(block.at[pl.ds(cell, run)], field.at[x, pl.ds(y, run)])
                cell += run
    for moved in copies[:speeds]:
        moved.wait()

    edges = brick_edges()
    for side, (first, last) in enumerate(((0, DEPTH), (16 + DEPTH, SPAN))):

        @pl.when(edges[side])
        def _(first=first, last=last):
            speed[:, first:last] = jnp.zeros((3, last - first, 32, 128), jnp.float32)

        @pl.when(edges[2 + side])
        def _(first=first, last=last):
            shift = ORIGIN - DEPTH
            speed[:, :, first + shift : last + shift] = jnp.zeros(
                (3, SPAN, last - first, 128), jnp.float32
            )

    def coefficients(x, carry):
        fill_coefficients(speed, coef, x, ORIGIN - REACH + 1, ORIGIN + 16 + REACH - 1)
        return carry

    lax.fori_loop(DEPTH - REACH + 1, DEPTH + 16 + REACH - 1, coefficients, 0)

    at_class = lax.broadcasted_iota(jnp.int32, (GROUP, 128), 0)
    rates = []
    for g in range(GROUPS):
        value = jnp.zeros((GROUP, 128), jnp.float32)
        for i in range(GROUP):
            value = jnp.where(at_class == i, -rate[g * GROUP + i], value)
        rates.append(value)
    low, high = DEPTH - REACH, DEPTH + 16 + REACH
    load[low:DEPTH, low:high, :] = above[0, :, 0 : high - low, :]
    load[DEPTH + 16 : high, low:high, :] = above[1, :, 0 : high - low, :]
    load[DEPTH : DEPTH + 16, low:DEPTH, :] = beside_low[...]
    load[DEPTH : DEPTH + 16, DEPTH : DEPTH + 16, :] = attach[...]
    load[DEPTH : DEPTH + 16, DEPTH + 16 : high, :] = beside_high[...]
    for moved in copies[speeds:]:
        moved.wait()

    def scale_row(reach, x, source, target, live):
        for y in range(DEPTH - reach, DEPTH + 16 + reach):
            kill = live
            if y < DEPTH:
                kill = kill & ~edges[2]
            elif y >= DEPTH + 16:
                kill = kill & ~edges[3]
            kill = kill.astype(jnp.float32)
            loaded = load[x, y : y + 1, :]
            for g in range(GROUPS):
                at = (x, y, slice(g * GROUP, (g + 1) * GROUP))
                scale = jnp.exp(rates[g] * loaded) * kill
                factor[at] = scale
                target[at] = source[at] * scale

    def step_row(step, reach, x, source, target, live):
        if step == 0:
            scale_row(reach, x, source, target, live)
            return

        def finish(at, value):
            return target, at, value * factor[at]

        first, last = DEPTH - reach, DEPTH + 16 + reach
        move_row(source, coef, x, first, last, ORIGIN - DEPTH, finish)

    source, target = field, other
    for step in range(DEPTH):
        reach = REACH - step

        def middle_rows(i, carry, step=step, reach=reach, source=source, target=target):
            for x in (DEPTH + 2 * i, DEPTH + 2 * i + 1):
                step_row(step, reach, x, source, target, jnp.bool_(True))
            return carry

        if step < DEPTH - 1:
            lax.fori_loop(0, 8, middle_rows, 0)
        else:
            for part in range(0, 16, PART):
                lax.fori_loop(part // 2, (part + PART) // 2, middle_rows, 0)
                for k in range(32):
                    pltpu.make_async_copy(
                        target.at[pl.ds(DEPTH + part, PART), inner, k],
                        out.at[k, pl.ds(part, PART)],
                        out_sem,
                    ).start()
        for away in range(1, reach + 1):

            def outer(i, carry, away=away, step=step, reach=reach, source=source, target=target):
                x = DEPTH - away + i * (15 + 2 * away)
                live = ~jnp.where(i == 0, edges[0], edges[1])
                step_row(step, reach - away, x, source, target, live)
                return carry

            lax.fori_loop(0, 2, outer, 0)
        source, target = target, source
    pltpu.make_async_copy(out, out, out_sem).wait()


def transported(*operands):
    vmem = pl.BlockSpec(memory_space=pltpu.VMEM)
    anywhere = pl.BlockSpec(memory_space=pl.ANY)
    return pl.pallas_call(
        transport_kernel,
        out_shape=jax.ShapeDtypeStruct((32, 16, 16, 128), jnp.float32),
        in_specs=[anywhere] * 12 + [pl.BlockSpec(memory_space=pltpu.SMEM)] + [vmem] * 3,
        out_specs=anywhere,
        scratch_shapes=[
            pltpu.VMEM((SPAN, SPAN, 32, 128), jnp.float32),
            pltpu.VMEM((SPAN, SPAN, 32, 128), jnp.float32),
            pltpu.VMEM((SPAN, SPAN, 32, 128), jnp.float32),
            pltpu.VMEM((3, SPAN, 32, 128), jnp.float32),
            pltpu.VMEM((7, SPAN, 32, 128), jnp.float32),
            pltpu.VMEM((SPAN, SPAN, 128), jnp.float32),
            pltpu.VMEM((2, REACH, 32, 128), jnp.float32),
            pltpu.SemaphoreType.DMA((1 + 6 * REACH + 6 + 2 + 12 * (REACH - 1) + 5 + 4 * (REACH - 1),)),
            pltpu.SemaphoreType.DMA,
        ],
        compiler_params=params(),
    )(*operands)


def body(
    classes,
    velocity,
    attach_rate,
    bubble_pos,
    bubble_volume,
    bubble_area,
    bubble_count,
    cluster_target,
    cluster_offset,
):
    devices = lax.axis_size("wide") * lax.axis_size("narrow")
    edge = edges_of(classes, velocity)
    *edge, bubble_volume = lax.optimization_barrier((*edge, bubble_volume))
    sent = pack(
        cluster_target.T,
        bubble_count.T,
        cluster_offset.T,
        jnp.transpose(bubble_pos, (1, 0, 2)),
        bubble_volume,
        bubble_area,
        devices,
    )
    side_low, side_high = rolled(edge[3], 0, 1), rolled(edge[2], 0, -1)
    wide_low, wide_high = rolled(edge[1], 1, 0), rolled(edge[0], -1, 0)
    sent, side_low, side_high, wide_low, wide_high = lax.optimization_barrier(
        (sent, side_low, side_high, wide_low, wide_high)
    )
    got = lax.all_to_all(sent, AXES, split_axis=0, concat_axis=0, tiled=True)
    own, *edge = first_moved(classes, velocity, wide_low, wide_high, side_low, side_high)
    got, own, *edge = lax.optimization_barrier((got, own, *edge))
    aside_low, aside_high = rolled(edge[3], 0, 1), rolled(edge[2], 0, -1)
    out_low, out_high = rolled(edge[1], 1, 0), rolled(edge[0], -1, 0)

    deposit, attach = deposited(got)
    attach, aside_low, aside_high = lax.optimization_barrier((attach, aside_low, aside_high))
    beside_low = rolled(attach[:, -REACH:], 0, 1)
    beside_high = rolled(attach[:, :REACH], 0, -1)
    turn_down, turn_up = turns(
        aside_low, aside_high, side_low, side_high, attach, beside_low, beside_high
    )
    turn_low, turn_high = rolled(turn_up, 1, 0), rolled(turn_down, -1, 0)
    return deposit, transported(
        own, velocity, out_low, out_high, aside_low, aside_high,
        wide_low, wide_high, side_low, side_high, turn_low, turn_high,
        attach_rate, attach, beside_low, beside_high,
    )


def solution(mesh):
    return jax.shard_map(
        body,
        mesh=mesh,
        in_specs=(
            P(None, "wide", "narrow", None),
            P(None, "wide", "narrow", None),
            P(),
            P(("wide", "narrow"), None, None),
            P(("wide", "narrow"), None),
            P(("wide", "narrow"), None),
            P(("wide", "narrow"), None),
            P(("wide", "narrow"), None),
            P(("wide", "narrow"), None),
        ),
        out_specs=(P(None, "wide", "narrow", None), P(None, "wide", "narrow", None)),
        check_vma=False,
    )
```

```python
import functools

import jax
import jax.numpy as jnp
from jax import lax
from jax.experimental import pallas as pl
from jax.experimental.pallas import tpu as pltpu
from jax.sharding import PartitionSpec as P

WIN = 4
DEPTH = 4
REACH = DEPTH - 1
GROUP = 8
AXES = ("wide", "narrow")
VMEM_BYTES = 60 * 1024 * 1024

CORNER = [(a, b) for a in range(REACH - 1) for b in range(REACH - 1 - a)]


def params(**more):
    return pltpu.CompilerParams(vmem_limit_bytes=VMEM_BYTES, **more)


def rolled(block, wide_step, narrow_step):
    wide_count, narrow_count = lax.axis_size("wide"), lax.axis_size("narrow")
    pairs = [
        (
            w * narrow_count + n,
            (w + wide_step) % wide_count * narrow_count + (n + narrow_step) % narrow_count,
        )
        for w in range(wide_count)
        for n in range(narrow_count)
    ]
    return lax.ppermute(block, AXES, pairs)


def wide_speed(i, d):
    return 16 + 2 * i + d // 2, pl.ds(16 * (d % 2), 16)


def edges_kernel(
    classes, velocity, wide_low, wide_high, side_low, side_high, field, speed, sem
):
    copies = []

    def copy(source, target):
        moved = pltpu.make_async_copy(source, target, sem.at[len(copies)])
        moved.start()
        copies.append(moved)

    copy(velocity, speed)
    for x, row in ((0, 0), (15, 1)):
        for k in range(32):
            copy(classes.at[k, x], field.at[row, :, k])
    aside = len(copies)
    for first in (0, 1):
        for k in range(32):
            copy(classes.at[k, :, pl.ds(8 * first, 8)], field.at[pl.ds(2, 16), pl.ds(8 * first, 8), k])
    for moved in copies[:aside]:
        moved.wait()
    leaving = len(copies)
    for out, row, first in ((wide_low, 0, 0), (wide_high, 1, 16 - REACH)):
        copy(field.at[row], out.at[pl.ds(0, 16)])
        for i in range(REACH):
            for d in range(3):
                copy(speed.at[d, first + i], out.at[wide_speed(i, d)])
    for out, y in ((side_low, 0), (side_high, 15)):
        for d in range(3):
            copy(speed.at[d, :, pl.ds(y // 8 * 8, 8)], out.at[:, 1, pl.ds(8 * d, 8)])
    for moved in copies[aside:leaving]:
        moved.wait()
    for out, y in ((side_low, 0), (side_high, 15)):
        copy(field.at[pl.ds(2, 16), y], out.at[:, 0])
    for moved in copies[leaving:]:
        moved.wait()


def edges_of(classes, velocity):
    anywhere = pl.BlockSpec(memory_space=pl.ANY)
    return pl.pallas_call(
        edges_kernel,
        out_shape=(jax.ShapeDtypeStruct((16 + 2 * REACH, 32, 128), jnp.float32),) * 2
        + (jax.ShapeDtypeStruct((16, 2, 32, 128), jnp.float32),) * 2,
        in_specs=[anywhere] * 2,
        out_specs=(anywhere,) * 4,
        scratch_shapes=[
            pltpu.VMEM((18, 16, 32, 128), jnp.float32),
            pltpu.VMEM((3, 16, 16, 128), jnp.float32),
            pltpu.SemaphoreType.DMA((129 + 8 + 2 + 6 * REACH,)),
        ],
        compiler_params=params(),
    )(classes, velocity)


def pack_kernel(target_of, count_of, corner_of, pos, volume, area, sent, tally):
    _, clusters, bubbles = pos.shape
    devices = sent.shape[0]
    row = count_of.shape[0]
    sent[...] = jnp.zeros_like(sent)

    def clear(d, carry):
        tally[d] = 0
        return carry

    lax.fori_loop(0, devices, clear, 0, unroll=8)
    lane = lax.broadcasted_iota(jnp.int32, (1, bubbles), 1)

    def some(r, carry):
        for i in range(row):
            c = r * row + i
            target, count = target_of[0, c], count_of[i, r]
            corner_x = corner_of[0, c].astype(jnp.float32)
            corner_y = corner_of[1, c].astype(jnp.float32)
            rank = tally[target]
            tally[target] = rank + 1
            live = lane < count
            at = pl.ds(c, 1)
            rows = [
                pos[0, at, :] * 4.0,
                pos[1, at, :] * 4.0,
                pos[2, at, :] * 128.0,
                jnp.where(live, volume[at, :], 0.0),
                jnp.where(live, area[at, :], 0.0),
            ]
            for j, value in enumerate(rows):
                start = pl.multiple_of((rank * 5 + j) * bubbles, bubbles)
                sent[target, :, pl.ds(start, bubbles)] = value
            tail = sent[target, :, pl.ds(10 * bubbles, bubbles)]
            tail = jnp.where(lane == 2 * rank, corner_x, tail)
            tail = jnp.where(lane == 2 * rank + 1, corner_y, tail)
            sent[target, :, pl.ds(10 * bubbles, bubbles)] = tail
        return carry

    lax.fori_loop(0, clusters // row, some, 0)


def pack(target_of, count_of, corner_of, pos, volume, area, devices):
    bubbles = pos.shape[2]
    return pl.pallas_call(
        pack_kernel,
        out_shape=jax.ShapeDtypeStruct((devices, 1, 11 * bubbles), jnp.float32),
        in_specs=[pl.BlockSpec(memory_space=pltpu.SMEM)] * 3
        + [pl.BlockSpec(memory_space=pltpu.VMEM)] * 3,
        out_specs=pl.BlockSpec(memory_space=pltpu.VMEM),
        scratch_shapes=[pltpu.SMEM((devices,), jnp.int32)],
        compiler_params=params(),
    )(target_of, count_of, corner_of, pos, volume, area)


UNROLL = 32


def halves(value):
    high = value.astype(jnp.bfloat16)
    return high, (value - high.astype(jnp.float32)).astype(jnp.bfloat16)


def across(left, right):
    return lax.dot_general(
        left, right, (((1,), (1,)), ((), ())), preferred_element_type=jnp.float32
    )


def bell(distance):
    return jnp.exp2((distance * (-0.5 * 1.4426950408889634)) * distance)


def deposit_kernel(got_any, got, deposit, attach, total, corners, sem):
    devices = got.shape[0]
    bubbles = got.shape[2] // 11
    copy = pltpu.make_async_copy(
        got_any.at[:, :, pl.ds(10 * bubbles, bubbles)], corners, sem
    )
    copy.start()
    total[...] = jnp.zeros_like(total)
    copy.wait()
    row = lax.broadcasted_iota(jnp.int32, (8, bubbles), 0)
    is_volume = row % 2 == 0
    cell_y = (row // 2).astype(jnp.float32) + 0.5
    cell_z = lax.broadcasted_iota(jnp.int32, (128, bubbles), 0).astype(jnp.float32) + 0.5

    def sources(step, carry):
        done = []
        for u in range(UNROLL):
            for slot in range(2):
                source = step * UNROLL + u
                px, py, pz, vol, are = (
                    got[source, :, (5 * slot + i) * bubbles : (5 * slot + i + 1) * bubbles]
                    for i in range(5)
                )
                share = bell(cell_y - py) * jnp.where(is_volume, vol, are)
                plane = jnp.concatenate(
                    [share * bell((i + 0.5) - px) for i in range(WIN)], axis=0
                )
                plane_high, plane_low = halves(plane)
                high, low = halves(bell(cell_z - pz))
                left = jnp.concatenate(
                    [
                        jnp.concatenate([plane_high, plane_high], axis=1),
                        jnp.concatenate([plane_low, jnp.zeros_like(plane_low)], axis=1),
                    ],
                    axis=0,
                )
                both = across(left, jnp.concatenate([high, low], axis=1))
                window = both[:32] + both[32:]
                done.append((source, slot, window))
        for source, slot, window in done:
            x = corners[source, 0, 2 * slot].astype(jnp.int32)
            y = corners[source, 0, 2 * slot + 1].astype(jnp.int32)
            for i in range(WIN):
                at = pl.ds((x + i) * 32 + y * 2, 8)
                total[at, :] = total[at, :] + window[8 * i : 8 * i + 8]
        return carry

    lax.fori_loop(0, devices // UNROLL, sources, 0)
    for x in range(16):
        gas = total[pl.ds(x * 32, 16, stride=2), :]
        face = total[pl.ds(x * 32 + 1, 16, stride=2), :]
        deposit[0, x] = gas
        deposit[1, x] = face
        attach[x] = face / (1.0 + gas)


def deposited(got):
    devices = got.shape[0]
    return pl.pallas_call(
        deposit_kernel,
        out_shape=(
            jax.ShapeDtypeStruct((2, 16, 16, 128), jnp.float32),
            jax.ShapeDtypeStruct((16, 16, 128), jnp.float32),
        ),
        in_specs=[
            pl.BlockSpec(memory_space=pl.ANY),
            pl.BlockSpec(memory_space=pltpu.VMEM),
        ],
        out_specs=(pl.BlockSpec(memory_space=pltpu.VMEM),) * 2,
        scratch_shapes=[
            pltpu.VMEM((520, 128), jnp.float32),
            pltpu.SMEM((devices, 1, 128), jnp.float32),
            pltpu.SemaphoreType.DMA,
        ],
        compiler_params=params(),
    )(got, got)


SPAN = 16 + 2 * DEPTH
ORIGIN = 8
BLOCK = 2
PART = 4
GROUPS = 32 // GROUP


def fill_coefficients(speed, coef, x, low, high):
    lane = lax.broadcasted_iota(jnp.int32, (high - low, 128), 1)

    def at(d, dx, dy):
        return speed[d, x + dx, low + dy : high + dy, :]

    middle = [at(d, 0, 0) for d in range(3)]
    left = 0.5 * (at(0, -1, 0) + middle[0])
    right = 0.5 * (middle[0] + at(0, 1, 0))
    kept = 1.0 - jnp.maximum(right, 0.0) + jnp.minimum(left, 0.0)
    coef[1, x, low:high, :] = jnp.maximum(left, 0.0)
    coef[2, x, low:high, :] = -jnp.minimum(right, 0.0)
    left = 0.5 * (at(1, 0, -1) + middle[1])
    right = 0.5 * (middle[1] + at(1, 0, 1))
    kept = kept - jnp.maximum(right, 0.0) + jnp.minimum(left, 0.0)
    coef[3, x, low:high, :] = jnp.maximum(left, 0.0)
    coef[4, x, low:high, :] = -jnp.minimum(right, 0.0)
    before = jnp.where(lane == 0, 0.0, pltpu.roll(middle[2], 1, 1))
    after = jnp.where(lane == 127, 0.0, pltpu.roll(middle[2], 127, 1))
    left, right = 0.5 * (before + middle[2]), 0.5 * (middle[2] + after)
    kept = kept - jnp.maximum(right, 0.0) + jnp.minimum(left, 0.0)
    coef[5, x, low:high, :] = jnp.where(lane == 0, 0.0, jnp.maximum(left, 0.0))
    coef[6, x, low:high, :] = jnp.where(lane == 127, 0.0, -jnp.minimum(right, 0.0))
    coef[0, x, low:high, :] = kept


def move_row(source, coef, x, first, last, to_speed, finish):
    def cell(dx, y, g):
        return source[x + dx, y, g * GROUP : (g + 1) * GROUP, :]

    before = [cell(0, first - 1, g) for g in range(GROUPS)]
    now = [cell(0, first, g) for g in range(GROUPS)]
    done = []
    for y in range(first, last):
        after = [cell(0, y + 1, g) for g in range(GROUPS)]
        yv = y + to_speed
        k = [jnp.broadcast_to(coef[i, x, yv : yv + 1, :], (GROUP, 128)) for i in range(7)]
        for g in range(GROUPS):
            value = k[0] * now[g]
            value = value + k[1] * cell(-1, y, g)
            value = value + k[2] * cell(1, y, g)
            value = value + k[3] * before[g]
            value = value + k[4] * after[g]
            value = value + k[5] * pltpu.roll(now[g], 1, 1)
            value = value + k[6] * pltpu.roll(now[g], 127, 1)
            done.append(finish((x, y, slice(g * GROUP, (g + 1) * GROUP)), value))
        before, now = now, after
        if (y - first) % BLOCK == BLOCK - 1 or y == last - 1:
            for ref, at, value in done:
                ref[at] = value
            done = []


def brick_edges():
    wide_at, narrow_at = lax.axis_index("wide"), lax.axis_index("narrow")
    wide_last, narrow_last = lax.axis_size("wide") - 1, lax.axis_size("narrow") - 1
    return wide_at == 0, wide_at == wide_last, narrow_at == 0, narrow_at == narrow_last


def first_kernel(
    classes, velocity, wide_low, wide_high, side_low, side_high,
    own, out_low, out_high, aside_low, aside_high,
    field, moved, speed, coef, sem,
):
    copies = []

    def copy(source, target):
        one = pltpu.make_async_copy(source, target, sem.at[len(copies)])
        one.start()
        copies.append(one)

    inner = pl.ds(1, 16)
    copy(velocity, speed.at[:, inner, pl.ds(ORIGIN, 16)])
    for d in range(3):
        copy(wide_low.at[wide_speed(REACH - 1, d)], speed.at[d, 0, pl.ds(ORIGIN, 16)])
        copy(wide_high.at[wide_speed(0, d)], speed.at[d, 17, pl.ds(ORIGIN, 16)])
        copy(side_low.at[:, 1, pl.ds(8 * d, 8)], speed.at[d, inner, pl.ds(0, 8)])
        copy(side_high.at[:, 1, pl.ds(8 * d, 8)], speed.at[d, inner, pl.ds(ORIGIN + 16, 8)])
    speeds = len(copies)
    for k in range(32):
        copy(classes.at[k], field.at[inner, inner, k])
    copy(wide_low.at[pl.ds(0, 16)], field.at[0, inner])
    copy(wide_high.at[pl.ds(0, 16)], field.at[17, inner])
    copy(side_low.at[:, 0], field.at[inner, 0])
    copy(side_high.at[:, 0], field.at[inner, 17])
    for one in copies[:speeds]:
        one.wait()
    edges = brick_edges()
    row = jnp.zeros((18, 32, 128), jnp.float32)
    for at, x in ((0, 0), (1, 17)):

        @pl.when(edges[at])
        def _(x=x):
            for d in range(3):
                speed[d, x] = jnp.zeros((32, 128), jnp.float32)

    for at, y in ((2, 0), (3, ORIGIN + 16)):

        @pl.when(edges[at])
        def _(y=y):
            speed[:, :, y : y + 8] = jnp.zeros((3, 18, 8, 128), jnp.float32)

    def coefficients(x, carry):
        fill_coefficients(speed, coef, x, ORIGIN, ORIGIN + 16)
        return carry

    lax.fori_loop(1, 17, coefficients, 0)
    for one in copies[speeds:]:
        one.wait()
    for at, here in ((0, 0), (1, 17)):

        @pl.when(edges[at])
        def _(here=here):
            field[here] = row

        @pl.when(edges[2 + at])
        def _(here=here):
            field[:, here] = row

    def rows(i, carry):
        for x in (1 + 2 * i, 2 + 2 * i):

            def finish(at, value):
                return moved, (at[0] - 1, at[1] - 1, at[2]), value

            move_row(field, coef, x, 1, 17, ORIGIN - 1, finish)
        return carry

    lax.fori_loop(0, 8, rows, 0)
    started = len(copies)
    copy(moved.at[pl.ds(0, REACH)], out_low)
    copy(moved.at[pl.ds(16 - REACH, REACH)], out_high)
    copy(moved.at[:, pl.ds(0, REACH)], aside_low)
    copy(moved.at[:, pl.ds(16 - REACH, REACH)], aside_high)
    copy(moved, own)
    for one in copies[started:]:
        one.wait()


def first_moved(classes, velocity, *halos):
    anywhere = pl.BlockSpec(memory_space=pl.ANY)
    return pl.pallas_call(
        first_kernel,
        out_shape=(jax.ShapeDtypeStruct((16, 16, 32, 128), jnp.float32),)
        + (jax.ShapeDtypeStruct((REACH, 16, 32, 128), jnp.float32),) * 2
        + (jax.ShapeDtypeStruct((16, REACH, 32, 128), jnp.float32),) * 2,
        in_specs=[anywhere] * 6,
        out_specs=(anywhere,) * 5,
        scratch_shapes=[
            pltpu.VMEM((18, 18, 32, 128), jnp.float32),
            pltpu.VMEM((16, 16, 32, 128), jnp.float32),
            pltpu.VMEM((3, 18, 32, 128), jnp.float32),
            pltpu.VMEM((7, 18, 32, 128), jnp.float32),
            pltpu.SemaphoreType.DMA((13 + 36 + 5,)),
        ],
        compiler_params=params(),
    )(classes, velocity, *halos)


TURN = len(CORNER) + REACH - 1
TURN_CELLS = 2 * TURN + REACH


def turns_kernel(
    aside_low, aside_high, side_low, side_high, attach, beside_low, beside_high, low, high, sem
):
    copies = []
    for side, out in enumerate((low, high)):
        for at, (block, speeds) in enumerate(((aside_low, side_low), (aside_high, side_high))):
            cell = TURN * at
            for a in range(REACH - 1):
                x, cells = 15 - a if side else a, REACH - 1 - a
                first = 0 if at else REACH - cells
                copies.append((block.at[x, pl.ds(first, cells)], out.at[pl.ds(cell, cells)]))
                cell += cells
                copies.append((speeds.at[x, 1], out.at[TURN * at + len(CORNER) + a]))
    moved = [
        pltpu.make_async_copy(source, target, sem.at[i])
        for i, (source, target) in enumerate(copies)
    ]
    for one in moved:
        one.start()
    for first, out in ((0, low), (16 - REACH, high)):
        for i in range(REACH):
            out[2 * TURN + i, 0:REACH, :] = beside_low[first + i]
            out[2 * TURN + i, REACH : REACH + 16, :] = attach[first + i]
            out[2 * TURN + i, REACH + 16 : 2 * REACH + 16, :] = beside_high[first + i]
    for one in moved:
        one.wait()


def turns(*operands):
    anywhere = pl.BlockSpec(memory_space=pl.ANY)
    vmem = pl.BlockSpec(memory_space=pltpu.VMEM)
    return pl.pallas_call(
        turns_kernel,
        out_shape=(jax.ShapeDtypeStruct((TURN_CELLS, 32, 128), jnp.float32),) * 2,
        in_specs=[anywhere] * 4 + [vmem] * 3,
        out_specs=(vmem,) * 2,
        scratch_shapes=[pltpu.SemaphoreType.DMA((8 * (REACH - 1),))],
        compiler_params=params(),
    )(*operands)


def transport_kernel(
    own, velocity, out_low, out_high, aside_low, aside_high,
    wide_low, wide_high, side_low, side_high, turn_low, turn_high,
    rate, attach, beside_low, beside_high,
    out,
    field, other, factor, speed, coef, load, above, sem, out_sem,
):
    copies = []

    def copy(source, target):
        moved = pltpu.make_async_copy(source, target, sem.at[len(copies)])
        moved.start()
        copies.append(moved)

    inner = pl.ds(DEPTH, 16)
    copy(velocity, speed.at[:, inner, pl.ds(ORIGIN, 16)])
    for block, first in ((wide_low, DEPTH - REACH), (wide_high, 16 + DEPTH)):
        for i in range(REACH):
            for d in range(3):
                copy(
                    block.at[wide_speed(i, d)],
                    speed.at[d, first + i, pl.ds(ORIGIN, 16)],
                )
    for block, first in ((side_low, 0), (side_high, ORIGIN + 16)):
        for d in range(3):
            copy(block.at[:, 1, pl.ds(8 * d, 8)], speed.at[d, inner, pl.ds(first, 8)])
    for side, block in enumerate((turn_low, turn_high)):
        copy(block.at[pl.ds(2 * TURN, REACH)], above.at[side])
        for at, first in enumerate((0, ORIGIN + 16)):
            for a in range(REACH - 1):
                x = 16 + DEPTH + a if side else DEPTH - 1 - a
                for d in range(3):
                    copy(
                        block.at[TURN * at + len(CORNER) + a, pl.ds(8 * d, 8)],
                        speed.at[d, x, pl.ds(first, 8)],
                    )
    speeds = len(copies)
    copy(own, field.at[inner, inner])
    for block, first in ((out_low, DEPTH - REACH), (out_high, 16 + DEPTH)):
        copy(block, field.at[pl.ds(first, REACH), inner])
    for block, first in ((aside_low, DEPTH - REACH), (aside_high, 16 + DEPTH)):
        copy(block, field.at[inner, pl.ds(first, REACH)])
    for side, block in enumerate((turn_low, turn_high)):
        for at in range(2):
            cell = TURN * at
            for a in range(REACH - 1):
                x = 16 + DEPTH + a if side else DEPTH - 1 - a
                run = REACH - 1 - a
                y = 16 + DEPTH if at else DEPTH - run
                copy(block.at[pl.ds(cell, run)], field.at[x, pl.ds(y, run)])
                cell += run
    for moved in copies[:speeds]:
        moved.wait()

    edges = brick_edges()
    for side, (first, last) in enumerate(((0, DEPTH), (16 + DEPTH, SPAN))):

        @pl.when(edges[side])
        def _(first=first, last=last):
            speed[:, first:last] = jnp.zeros((3, last - first, 32, 128), jnp.float32)

        @pl.when(edges[2 + side])
        def _(first=first, last=last):
            shift = ORIGIN - DEPTH
            speed[:, :, first + shift : last + shift] = jnp.zeros(
                (3, SPAN, last - first, 128), jnp.float32
            )

    def coefficients(x, carry):
        fill_coefficients(speed, coef, x, ORIGIN - REACH + 1, ORIGIN + 16 + REACH - 1)
        return carry

    lax.fori_loop(DEPTH - REACH + 1, DEPTH + 16 + REACH - 1, coefficients, 0)

    at_class = lax.broadcasted_iota(jnp.int32, (GROUP, 128), 0)
    rates = []
    for g in range(GROUPS):
        value = jnp.zeros((GROUP, 128), jnp.float32)
        for i in range(GROUP):
            value = jnp.where(at_class == i, -rate[g * GROUP + i], value)
        rates.append(value)
    low, high = DEPTH - REACH, DEPTH + 16 + REACH
    load[low:DEPTH, low:high, :] = above[0, :, 0 : high - low, :]
    load[DEPTH + 16 : high, low:high, :] = above[1, :, 0 : high - low, :]
    load[DEPTH : DEPTH + 16, low:DEPTH, :] = beside_low[...]
    load[DEPTH : DEPTH + 16, DEPTH : DEPTH + 16, :] = attach[...]
    load[DEPTH : DEPTH + 16, DEPTH + 16 : high, :] = beside_high[...]
    for moved in copies[speeds:]:
        moved.wait()

    def scale_row(reach, x, source, target, live):
        for y in range(DEPTH - reach, DEPTH + 16 + reach):
            kill = live
            if y < DEPTH:
                kill = kill & ~edges[2]
            elif y >= DEPTH + 16:
                kill = kill & ~edges[3]
            kill = kill.astype(jnp.float32)
            loaded = load[x, y : y + 1, :]
            for g in range(GROUPS):
                at = (x, y, slice(g * GROUP, (g + 1) * GROUP))
                scale = jnp.exp(rates[g] * loaded) * kill
                factor[at] = scale
                target[at] = source[at] * scale

    def step_row(step, reach, x, source, target, live):
        if step == 0:
            scale_row(reach, x, source, target, live)
            return

        def finish(at, value):
            return target, at, value * factor[at]

        first, last = DEPTH - reach, DEPTH + 16 + reach
        move_row(source, coef, x, first, last, ORIGIN - DEPTH, finish)

    source, target = field, other
    for step in range(DEPTH):
        reach = REACH - step

        def middle_rows(i, carry, step=step, reach=reach, source=source, target=target):
            for x in (DEPTH + 2 * i, DEPTH + 2 * i + 1):
                step_row(step, reach, x, source, target, jnp.bool_(True))
            return carry

        if step < DEPTH - 1:
            lax.fori_loop(0, 8, middle_rows, 0)
        else:
            for part in range(0, 16, PART):
                lax.fori_loop(part // 2, (part + PART) // 2, middle_rows, 0)
                for k in range(32):
                    pltpu.make_async_copy(
                        target.at[pl.ds(DEPTH + part, PART), inner, k],
                        out.at[k, pl.ds(part, PART)],
                        out_sem,
                    ).start()
        for away in range(1, reach + 1):

            def outer(i, carry, away=away, step=step, reach=reach, source=source, target=target):
                x = DEPTH - away + i * (15 + 2 * away)
                live = ~jnp.where(i == 0, edges[0], edges[1])
                step_row(step, reach - away, x, source, target, live)
                return carry

            lax.fori_loop(0, 2, outer, 0)
        source, target = target, source
    pltpu.make_async_copy(out, out, out_sem).wait()


def transported(*operands):
    vmem = pl.BlockSpec(memory_space=pltpu.VMEM)
    anywhere = pl.BlockSpec(memory_space=pl.ANY)
    return pl.pallas_call(
        transport_kernel,
        out_shape=jax.ShapeDtypeStruct((32, 16, 16, 128), jnp.float32),
        in_specs=[anywhere] * 12 + [pl.BlockSpec(memory_space=pltpu.SMEM)] + [vmem] * 3,
        out_specs=anywhere,
        scratch_shapes=[
            pltpu.VMEM((SPAN, SPAN, 32, 128), jnp.float32),
            pltpu.VMEM((SPAN, SPAN, 32, 128), jnp.float32),
            pltpu.VMEM((SPAN, SPAN, 32, 128), jnp.float32),
            pltpu.VMEM((3, SPAN, 32, 128), jnp.float32),
            pltpu.VMEM((7, SPAN, 32, 128), jnp.float32),
            pltpu.VMEM((SPAN, SPAN, 128), jnp.float32),
            pltpu.VMEM((2, REACH, 32, 128), jnp.float32),
            pltpu.SemaphoreType.DMA((1 + 6 * REACH + 6 + 2 + 12 * (REACH - 1) + 5 + 4 * (REACH - 1),)),
            pltpu.SemaphoreType.DMA,
        ],
        compiler_params=params(),
    )(*operands)


def body(
    classes,
    velocity,
    attach_rate,
    bubble_pos,
    bubble_volume,
    bubble_area,
    bubble_count,
    cluster_target,
    cluster_offset,
):
    devices = lax.axis_size("wide") * lax.axis_size("narrow")
    edge = edges_of(classes, velocity)
    *edge, bubble_volume = lax.optimization_barrier((*edge, bubble_volume))
    sent = pack(
        cluster_target.T,
        bubble_count.T,
        cluster_offset.T,
        jnp.transpose(bubble_pos, (1, 0, 2)),
        bubble_volume,
        bubble_area,
        devices,
    )
    side_low, side_high = rolled(edge[3], 0, 1), rolled(edge[2], 0, -1)
    wide_low, wide_high = rolled(edge[1], 1, 0), rolled(edge[0], -1, 0)
    sent, side_low, side_high, wide_low, wide_high = lax.optimization_barrier(
        (sent, side_low, side_high, wide_low, wide_high)
    )
    got = lax.all_to_all(sent, AXES, split_axis=0, concat_axis=0, tiled=True)
    own, *edge = first_moved(classes, velocity, wide_low, wide_high, side_low, side_high)
    got, own, *edge = lax.optimization_barrier((got, own, *edge))
    aside_low, aside_high = rolled(edge[3], 0, 1), rolled(edge[2], 0, -1)
    out_low, out_high = rolled(edge[1], 1, 0), rolled(edge[0], -1, 0)

    deposit, attach = deposited(got)
    attach, aside_low, aside_high = lax.optimization_barrier((attach, aside_low, aside_high))
    beside_low = rolled(attach[:, -REACH:], 0, 1)
    beside_high = rolled(attach[:, :REACH], 0, -1)
    turn_down, turn_up = turns(
        aside_low, aside_high, side_low, side_high, attach, beside_low, beside_high
    )
    turn_low, turn_high = rolled(turn_up, 1, 0), rolled(turn_down, -1, 0)
    return deposit, transported(
        own, velocity, out_low, out_high, aside_low, aside_high,
        wide_low, wide_high, side_low, side_high, turn_low, turn_high,
        attach_rate, attach, beside_low, beside_high,
    )


def solution(mesh):
    return jax.shard_map(
        body,
        mesh=mesh,
        in_specs=(
            P(None, "wide", "narrow", None),
            P(None, "wide", "narrow", None),
            P(),
            P(("wide", "narrow"), None, None),
            P(("wide", "narrow"), None),
            P(("wide", "narrow"), None),
            P(("wide", "narrow"), None),
            P(("wide", "narrow"), None),
            P(("wide", "narrow"), None),
        ),
        out_specs=(P(None, "wide", "narrow", None), P(None, "wide", "narrow", None)),
        check_vma=False,
    )
```
